128 devices in a mesh: chain: 16 (over z, y), sector: 8 (over x, core).
Axes of the slice: x: 4, y: 4, z: 4, core: 2. Of those that a mesh axis runs over, the one named last changes fastest.
Arguments:
- theta: bfloat16 [16, 16, 16, 256, 256], P('chain', 'sector'), may hold values from -6 to 6
- env_left0: bfloat16 [16, 2, 256, 256], P('sector'), may hold values from -0.375 to 0.375
- transfer: float32 [16, 16, 256, 256], P('chain', 'sector')
- env_right: bfloat16 [16, 16, 2, 256, 256], P('chain', 'sector'), may hold values from -0.375 to 0.375
- mpo_weights: float32 [2, 16, 16], replicated, may hold values from -1.5 to 1.5
- term_mask: int32 [16, 2], P('sector'), may hold values 0 or 1
- block_sizes: int32 [16], P('sector'), may hold values from 64 to 256, as said below
- ritz: float32 [16, 4], P('chain'), may hold values from -4 to 4
Outputs:
- psi: float32 [16, 16, 16, 256, 256], P('chain', 'sector')
- tridiag: float32 [16, 2, 3], P('chain')
The draws below stay inside these ranges and needn't reach their ends.
Inputs may be any that keep to these rules, and one draw needn't show every extreme that they name: `block_sizes`: each size lies between 64 and 256; both ends occur in every draw.
All inputs are finite; a program needn't handle non-finite values. No bound on the sum of `term_mask` on one device may be relied on, other than what follows from the above.
Results may differ from the reference program's by a relative error of at most 0.0075.
Values may be sent and summed in bfloat16 or wider, within the bound.
A program may use at most 192 MiB of HBM per device.

```python
import jax
import jax.numpy as jnp
import numpy as np
from jax import lax

P_SIZE = 16
BMAX = 256
K = 2
ITERS = 4
NSEC = 16
SITES = 16


def draw_transfer(key, part):
    shape = (SITES, NSEC, BMAX, BMAX)
    sign_key, noise_key = jax.random.split(jax.random.fold_in(key, 11))
    flips = jax.random.bernoulli(sign_key, 0.5, (SITES, NSEC, BMAX)).astype(jnp.float32)
    signs = 2.0 * flips - 1.0
    diag_part = 0.95 * signs[:, :, :, None] * jnp.eye(BMAX, dtype=jnp.float32)
    noise = 0.3 / BMAX ** 0.5 * jax.random.normal(noise_key, shape, jnp.float32)
    return noise + diag_part


def draw_block_sizes(key, part):
    first, second = jax.random.split(jax.random.fold_in(key, 7))
    sizes = jax.random.randint(first, (NSEC,), BMAX // 4, BMAX + 1).astype(jnp.int32)
    order = jax.random.permutation(second, NSEC)
    sizes = sizes.at[order[0]].set(BMAX).at[order[1]].set(BMAX // 4)
    return sizes.astype(jnp.int32)


def plant(values, key, low, top_value):
    longest = values.shape.index(max(values.shape))
    spots = []
    for shift in (0, 1):
        where = [jax.random.randint(jax.random.fold_in(key, axis), (), 0, length) for axis, length in enumerate(values.shape)]
        where[longest] = (where[longest] + shift) % values.shape[longest]
        spots.append(tuple(where))
    return values.at[spots[0]].set(low).at[spots[1]].set(top_value)


def steps_of(own_key, shape, shards, low, largest):
    loudness = 1.0
    for position, shards_of in shards:
        heights = jax.random.uniform(jax.random.fold_in(jax.random.fold_in(own_key, 6), position), (shards_of,), jnp.float32, low / len(shards), largest / len(shards))
        loudness = loudness * jnp.repeat(jnp.exp(heights), shape[position] // shards_of).reshape((-1,) + (1,) * (len(shape) - 1 - position))
    return loudness


def bell_draw(key, extent, scale, bound, cuts=(), kind=jnp.bfloat16):
    drawn = jax.random.normal(key, extent, jnp.float32) * scale
    if len(cuts) > 0:
        drawn = steps_of(key, extent, cuts, -0.22, 0.18) * drawn
    return jnp.clip(drawn, min=-bound, max=bound).astype(kind)


def setup_inputs(seed: int = 0) -> dict:
    key_list = jax.random.split(jax.random.key(seed), 9)
    theta = bell_draw(key_list[0], (SITES, NSEC, P_SIZE, BMAX, BMAX), 1.0, 6.0, ((0, 16), (1, 8)))
    env_left0 = bell_draw(key_list[1], (NSEC, K, BMAX, BMAX), BMAX ** -0.5, 0.375, ((0, 8),))
    transfer = draw_transfer(jax.random.fold_in(key_list[8], 71), 0)
    env_right = bell_draw(key_list[3], (SITES, NSEC, K, BMAX, BMAX), BMAX ** -0.5, 0.375, ((0, 16), (1, 8)))
    mpo_weights = bell_draw(key_list[4], (K, P_SIZE, P_SIZE), P_SIZE ** -0.5, 1.5, (), jnp.float32)
    term_mask = plant((jax.random.randint(key_list[5], (NSEC, K), 0, 4) < 3).astype(jnp.int32), jax.random.fold_in(key_list[5], 1), 0, 1)
    block_sizes = draw_block_sizes(jax.random.fold_in(key_list[8], 71), 0)
    ritz = bell_draw(key_list[7], (SITES, ITERS), 1.0, 4.0, ((0, 16),), jnp.float32)
    return dict(theta=theta, env_left0=env_left0, transfer=transfer, env_right=env_right, mpo_weights=mpo_weights, term_mask=term_mask, block_sizes=block_sizes, ritz=ritz)


charge_table = np.array([-2, -1, -1, -1, -1, 0, 0, 0, 0, 0, 0, 1, 1, 1, 1, 2])
group_bounds = [(0, 1), (1, 5), (5, 11), (11, 15), (15, 16)]
highest = lax.Precision.HIGHEST
eps = 1e-06

def apply_operator(vector, left_env, right_pad, mixing, gates):
    total = jnp.zeros(vector.shape, jnp.float32)
    count_sec = vector.shape[0]
    for term in range(mixing.shape[0]):
        mixed = jnp.einsum('pq,sqij->spij', mixing[term], vector, precision=highest).astype(jnp.bfloat16)
        upper = jnp.einsum('sik,spkj->spij', left_env[:, term].astype(jnp.float32), mixed.astype(jnp.float32)).astype(jnp.bfloat16)
        for level in range(5):
            begin, finish = group_bounds[level]
            picked = right_pad[level:level + count_sec, term].astype(jnp.float32)
            part = jnp.einsum('spij,slj->spil', upper[:, begin:finish].astype(jnp.float32), picked)
            total = total.at[:, begin:finish].add(gates[:, term][:, None, None, None] * part)
    return total

def reference(theta, env_left0, transfer, env_right, mpo_weights, term_mask, block_sizes, ritz):
    width = theta.shape[-1]
    live = (jnp.arange(width)[None, :] < block_sizes[:, None]).astype(jnp.float32)
    box_mask = live[:, :, None] * live[:, None, :]
    same = (charge_table[:, None] == charge_table[None, :]).astype(np.float32)
    mixing = mpo_weights * jnp.asarray(same, jnp.float32)
    gates = term_mask.astype(jnp.float32)
    left_base = env_left0.astype(jnp.float32) * box_mask[:, None]
    nsec_all = theta.shape[1]
    count = float(nsec_all * theta.shape[2] * width * width)
    prefix = jnp.broadcast_to(jnp.eye(width, dtype=jnp.float32), box_mask.shape)
    psi_list = []
    tri_list = []
    for site in range(theta.shape[0]):
        factor = transfer[site] * box_mask
        inner = jnp.einsum('swjk,skl->swjl', left_base, prefix, precision=highest)
        left_env = jnp.einsum('sji,swjl->swil', prefix, inner, precision=highest).astype(jnp.bfloat16)
        right_env = env_right[site] * box_mask[:, None].astype(jnp.bfloat16)
        right_pad = jnp.pad(right_env, ((2, 2), (0, 0), (0, 0), (0, 0)))
        start = theta[site].astype(jnp.float32) * box_mask[:, None]
        vectors = [start / jnp.sqrt(jnp.sum(start * start) / count + eps)]
        alphas = []
        betas = []
        for step in range(ITERS - 1):
            image = apply_operator(vectors[-1], left_env, right_pad, mixing, gates)
            alpha = jnp.sum(vectors[-1] * image) / count
            image = image - alpha * vectors[-1]
            if step > 0:
                image = image - betas[-1] * vectors[-2]
            beta = jnp.sqrt(jnp.sum(image * image) / count + eps)
            vectors.append(image / beta)
            alphas.append(alpha)
            betas.append(beta)
        combined = jnp.zeros(start.shape, jnp.float32)
        for index in range(ITERS):
            combined = combined + ritz[site, index] * vectors[index]
        psi_list.append(combined)
        tri_list.append(jnp.stack([jnp.stack(alphas), jnp.stack(betas)]))
        prefix = jnp.einsum('sij,sjk->sik', prefix, factor, precision=highest)
    return (jnp.stack(psi_list), jnp.stack(tri_list))
```

```python
import functools

import jax
import jax.numpy as jnp
from jax import lax
from jax.experimental import pallas as pl
from jax.experimental.pallas import tpu as pltpu
from jax.sharding import PartitionSpec as P

f32, bf16 = jnp.float32, jnp.bfloat16
MESH = pl.DeviceIdType.MESH
group_bounds = [(0, 1), (1, 5), (5, 11), (11, 15), (15, 16)]
eps = 1e-6
LINE = 4
TOP = 32767.0


def split(x):
    high = x.astype(bf16)
    return high, (x - high.astype(f32)).astype(bf16)


def mm(a, b):
    return jnp.dot(a, b, preferred_element_type=f32)


def mm_nt(a, b):
    return lax.dot_general(a, b, (((1,), (1,)), ((), ())), preferred_element_type=f32)


def mm3(a, b):
    return mm(a[0], b[0]) + mm(a[0], b[1]) + mm(a[1], b[0])


def encode(x, ref):
    n = x.shape[0]
    top = jnp.max(jnp.abs(x), axis=0, keepdims=True)
    power = jnp.ceil(jnp.log2(jnp.maximum(top, 1e-35)) + 0.01)
    code = jnp.round(x * (jnp.exp2(-power) * TOP))
    ref[0:n] = code.astype(jnp.int32).astype(jnp.int16)
    ref[n : n + 16] = jnp.broadcast_to(power, (16, x.shape[1])).astype(jnp.int32).astype(jnp.int16)


def decode(ref):
    n = ref.shape[0] - 16
    power = ref[n : n + 16].astype(jnp.int32).astype(f32)[0:1]
    return ref[0:n].astype(jnp.int32).astype(f32) * (jnp.exp2(power) * (1.0 / TOP))


def fold(x):
    return jnp.sum(x.reshape(-1, 8, x.shape[-1]), axis=0)


def kernel(
    sizes, gates, ritz, theta, env_left, transfer, env_right, weights,
    u_out, w0_out, w1_out, w2_out, tri_out, coef_out,
    gbuf, tbuf, rbuf, wk, env, ypre, u, w0, w1, w2, mixed, half, ex_src, ex_dst,
    theta_sem, out_sem, g_send, g_recv, t_send, t_recv, r_send, r_recv, e_send, e_recv,
):
    nsec, nstate, n = u.shape[0], u.shape[1], u.shape[-1]
    chain, sector = lax.axis_index("chain"), lax.axis_index("sector")
    peers = ex_dst.shape[1]
    count = float(peers * nsec * nstate * n * n)
    z, y = chain // LINE, lax.rem(chain, LINE)

    theta_copy = pltpu.make_async_copy(theta.at[0], u, theta_sem)
    theta_copy.start()

    def on_y(d):
        return (z * LINE + lax.rem(y + d, LINE), sector)

    def on_z(d):
        return (lax.rem(z + d, LINE) * LINE + y, sector)

    def on_sector(d):
        return (chain, lax.rem(sector + d, peers))

    barrier = pltpu.get_barrier_semaphore()
    others = [on_y(1), on_y(LINE - 1), on_z(1), on_z(LINE - 1)] + [on_sector(d) for d in range(1, peers)]
    for other in others:
        pl.semaphore_signal(barrier, inc=1, device_id=other, device_id_type=MESH)

    rows = lax.broadcasted_iota(jnp.int32, (n, n), 0)
    cols = lax.broadcasted_iota(jnp.int32, (n, n), 1)

    def mask_of(s):
        return jnp.where((rows < sizes[s]) & (cols < sizes[s]), 1.0, 0.0).astype(f32)

    for s in range(nsec):
        mask = mask_of(s)
        encode(transfer[0, s] * mask, gbuf.at[0, s])
        for w in range(2):
            rbuf[2 + s, w] = (env_right[0, s, w].astype(f32) * mask).astype(bf16)
    pl.semaphore_wait(barrier, len(others))

    def remote(src, dst, send, recv, device):
        copy = pltpu.make_async_remote_copy(
            src_ref=src, dst_ref=dst, send_sem=send, recv_sem=recv,
            device_id=device, device_id_type=MESH,
        )
        copy.start()
        return copy

    def gather_start(buf, send, recv, onward, back):
        right0 = remote(buf.at[0, 0], buf.at[1, 0], send.at[0], recv.at[0], onward)
        left1 = remote(buf.at[0, 1], buf.at[3, 1], send.at[1], recv.at[1], back)
        right1 = remote(buf.at[0, 1], buf.at[1, 1], send.at[2], recv.at[2], onward)
        left0 = remote(buf.at[0, 0], buf.at[3, 0], send.at[3], recv.at[3], back)
        return right0, left1, right1, left0

    def gather_forward(copies, buf, send, recv, onward, back):
        copies[0].wait_recv()
        far0 = remote(buf.at[1, 0], buf.at[2, 0], send.at[4], recv.at[4], onward)
        copies[1].wait_recv()
        far1 = remote(buf.at[3, 1], buf.at[2, 1], send.at[5], recv.at[5], back)
        return copies + (far0, far1)

    def gather_finish(copies):
        for copy in copies[2:]:
            copy.wait_recv()
        for copy in copies:
            copy.wait_send()

    def exchange_start(e, sums):
        for i, x in enumerate(sums):
            ex_src[e, i] = x[:, :128] + x[:, 128:]
        for i in range(len(sums), ex_src.shape[1]):
            ex_src[e, i] = jnp.zeros((8, 128), f32)
        ex_dst[e, sector] = ex_src[e]
        return [
            remote(ex_src.at[e], ex_dst.at[e, sector], e_send.at[e, d], e_recv.at[e, d], on_sector(d))
            for d in range(1, peers)
        ]

    def exchange_finish(e, copies, amount):
        for copy in copies:
            copy.wait_recv()
        for copy in copies:
            copy.wait_send()
        total = ex_dst[e, 0]
        for d in range(1, peers):
            total = total + ex_dst[e, d]
        return [jnp.sum(jnp.sum(total[i], axis=0, keepdims=True), axis=1, keepdims=True) for i in range(amount)]

    def mix(src, s):
        def step(i, _):
            span = pl.ds(pl.multiple_of(i * 16, 16), 16)
            block = src[s, :, span, :].reshape(nstate * 16, n)
            out = mm(wk[...], block).astype(bf16).reshape(2, nstate, 16, n)
            mixed[s, :, :, span, :] = out
            return 0

        lax.fori_loop(0, n // 16, step, 0, unroll=True)

    def right_side(s):
        for level, (begin, finish) in enumerate(group_bounds):
            for w in range(2):
                def step(p, _):
                    half[s, p, w * n : (w + 1) * n, :] = mm_nt(mixed[s, w, p], rbuf[s + level, w]).astype(bf16)
                    return 0

                lax.fori_loop(begin, finish, step, 0, unroll=True)

    def both(f):
        def step(s, _):
            f(s)
            return 0

        lax.fori_loop(0, nsec, step, 0)

    def left_side(finish, sums):
        zero = tuple(jnp.zeros((8, n), f32) for _ in range(sums))

        def on_sec(s, accs):
            def on_state(p, accs):
                values = finish(s, p, mm(env[s], half[s, p]))
                return tuple(a + fold(v) for a, v in zip(accs, values))

            return lax.fori_loop(0, nstate, on_state, accs, unroll=True)

        return lax.fori_loop(0, nsec, on_sec, zero)

    ring_y = (on_y(1), on_y(LINE - 1))
    ring_z = (on_z(1), on_z(LINE - 1))
    copies = gather_start(gbuf, g_send, g_recv, *ring_y)
    halo = (
        remote(rbuf.at[pl.ds(2, 2)], rbuf.at[pl.ds(0, 2)], r_send.at[0], r_recv.at[0], on_sector(1)),
        remote(rbuf.at[pl.ds(2, 2)], rbuf.at[pl.ds(4, 2)], r_send.at[1], r_recv.at[1], on_sector(peers - 1)),
    )

    def charge(p):
        return sum((p >= bound).astype(jnp.int32) for bound in (1, 5, 11, 15))

    shape = (2 * nstate, nstate)
    state_row = lax.broadcasted_iota(jnp.int32, shape, 0) % nstate
    state_col = lax.broadcasted_iota(jnp.int32, shape, 1)
    table = jnp.where(charge(state_row) == charge(state_col), weights[...], 0.0).astype(bf16)
    tall = (2 * nstate * 16, 2 * nstate)
    spread_rows = jnp.where(
        lax.broadcasted_iota(jnp.int32, tall, 0) // 16 == lax.broadcasted_iota(jnp.int32, tall, 1), 1.0, 0.0
    ).astype(bf16)
    wide = (nstate, nstate * 16)
    spread_cols = jnp.where(
        lax.broadcasted_iota(jnp.int32, wide, 1) // 16 == lax.broadcasted_iota(jnp.int32, wide, 0), 1.0, 0.0
    ).astype(bf16)
    full = mm(mm(spread_rows, table).astype(bf16), spread_cols)
    big = full.shape
    same = lax.broadcasted_iota(jnp.int32, big, 0) % 16 == lax.broadcasted_iota(jnp.int32, big, 1) % 16
    wk[...] = jnp.where(same, full, 0.0).astype(bf16)

    theta_copy.wait()

    def masked(s, acc):
        mask = mask_of(s)

        def step(p, acc):
            value = u[s, p].astype(f32) * mask
            u[s, p] = value.astype(bf16)
            return acc + fold(value * value)

        return lax.fori_loop(0, nstate, step, acc, unroll=2)

    square = lax.fori_loop(0, nsec, masked, jnp.zeros((8, n), f32))
    started = exchange_start(0, [square])
    u_copy = pltpu.make_async_copy(u, u_out, out_sem.at[0])
    u_copy.start()
    mix(u, 0)
    copies = gather_forward(copies, gbuf, g_send, g_recv, *ring_y)
    mix(u, 1)
    gather_finish(copies)

    def slot(buf, at, j, s):
        return decode(buf.at[lax.rem(at - j + LINE, LINE), s])

    seconds = []
    for s in range(nsec):
        factors = [split(slot(gbuf, y, j, s)) for j in range(LINE)]
        second = mm3(factors[0], factors[1])
        later = mm3(factors[2], factors[3])
        ypre[s] = second
        encode(mm3(split(second), split(later)), tbuf.at[0, s])
    copies = gather_start(tbuf, t_send, t_recv, *ring_z)

    eye = jnp.where(rows == cols, 1.0, 0.0).astype(f32)

    def chosen(at, values):
        return jnp.where(
            at == 0, eye, jnp.where(at == 1, values[0], jnp.where(at == 2, values[1], values[2]))
        )

    for s in range(nsec):
        second = ypre[s]
        third = mm3(split(second), split(slot(gbuf, y, 2, s)))
        ypre[s] = chosen(y, (slot(gbuf, y, 0, s), second, third))
    for copy in halo:
        copy.wait()

    @pl.when(sector == 0)
    def _():
        rbuf[0:2] = jnp.zeros_like(rbuf[0:2])

    @pl.when(sector == peers - 1)
    def _():
        rbuf[4:6] = jnp.zeros_like(rbuf[4:6])

    (uu,) = exchange_finish(0, started, 1)
    right_side(0)
    copies = gather_forward(copies, tbuf, t_send, t_recv, *ring_z)
    right_side(1)
    gather_finish(copies)

    for s in range(nsec):
        first = slot(tbuf, z, 0, s)
        second = mm3(split(first), split(slot(tbuf, z, 1, s)))
        third = mm3(split(second), split(slot(tbuf, z, 2, s)))
        prefix = mm3(split(chosen(z, (first, second, third))), split(ypre[s]))
        high, low = split(prefix)
        high_t, low_t = split(prefix.T)
        mask = mask_of(s)
        for w in range(2):
            base = (env_left[s, w].astype(f32) * mask).astype(bf16)
            inner = split(mm(base, high) + mm(base, low))
            left = mm3((high_t, low_t), inner).astype(bf16).astype(f32) * gates[s, w].astype(f32)
            env[s, :, w * n : (w + 1) * n] = left.astype(bf16)

    def scalar(x):
        return x[0, 0]

    c0 = 1.0 / jnp.sqrt(uu / count + eps)
    c0_s = scalar(c0)

    def finish0(s, p, image):
        value = image * c0_s
        w0[s, p] = value.astype(bf16)
        return value * u[s, p].astype(f32), value * value

    started = exchange_start(1, left_side(finish0, 2))
    w0_copy = pltpu.make_async_copy(w0, w0_out, out_sem.at[1])
    w0_copy.start()
    both(lambda s: mix(w0, s))
    both(right_side)
    s1, s2 = exchange_finish(1, started, 2)

    def inverse(x):
        return 1.0 / x

    def root(x):
        return jnp.sqrt(jnp.maximum(x, 0.0) / count + eps)

    n00 = c0 * c0 * uu
    v0w0 = c0 * s1
    a0 = v0w0 / count
    r0 = s2 - 2.0 * a0 * v0w0 + a0 * a0 * n00
    b0 = root(r0)
    i0 = inverse(b0)
    n11 = r0 * i0 * i0
    n01 = (v0w0 - a0 * n00) * i0

    k_image, k_w0 = scalar(i0), scalar(a0 * i0)

    def finish1(s, p, image):
        before = w0[s, p].astype(f32)
        value = image * k_image - before * k_w0
        w1[s, p] = value.astype(bf16)
        return value * u[s, p].astype(f32), value * before, value * value

    started = exchange_start(2, left_side(finish1, 3))
    w1_copy = pltpu.make_async_copy(w1, w1_out, out_sem.at[2])
    w1_copy.start()
    both(lambda s: mix(w1, s))
    both(right_side)
    d0, d1, d2 = exchange_finish(2, started, 3)
    v0w1 = c0 * d0
    v1w1 = (d1 - a0 * v0w1) * i0
    a1 = v1w1 / count
    r1 = d2 + a1 * a1 * n11 + b0 * b0 * n00 - 2.0 * a1 * v1w1 - 2.0 * b0 * v0w1 + 2.0 * a1 * b0 * n01
    b1 = root(r1)
    i1 = inverse(b1)
    n22 = r1 * i1 * i1
    n12 = (v1w1 - a1 * n11 - b0 * n01) * i1

    k_image2, k_w1, k_w02 = scalar(i1), scalar(a1 * i1), scalar(b0 * i1)

    def finish2(s, p, image):
        older, before = w0[s, p].astype(f32), w1[s, p].astype(f32)
        value = image * k_image2 - before * k_w1 - older * k_w02
        w2[s, p] = value.astype(bf16)
        return value * u[s, p].astype(f32), value * older, value * before, value * value

    started = exchange_start(3, left_side(finish2, 4))
    w2_copy = pltpu.make_async_copy(w2, w2_out, out_sem.at[3])
    w2_copy.start()
    f0, f1, f2, f3 = exchange_finish(3, started, 4)
    v0w2 = c0 * f0
    v1w2 = (f1 - a0 * v0w2) * i0
    v2w2 = (f2 - a1 * v1w2 - b0 * v0w2) * i1
    a2 = v2w2 / count
    r2 = f3 + a2 * a2 * n22 + b1 * b1 * n11 - 2.0 * a2 * v2w2 - 2.0 * b1 * v1w2 + 2.0 * a2 * b1 * n12
    b2 = root(r2)
    k3 = ritz[0, 3] / b2
    m2 = ritz[0, 2] - k3 * a2
    m1 = ritz[0, 1] - k3 * b1 - m2 * a1 * i1
    m0 = ritz[0, 0] - m2 * b0 * i1 - m1 * a0 * i0
    for i, x in enumerate((a0, a1, a2, b0, b1, b2)):
        tri_out[i : i + 1, :] = jnp.broadcast_to(x, (1, 128))
    for i, x in enumerate((m0 * c0, m1 * i0, m2 * i1, k3)):
        coef_out[i : i + 1, :] = jnp.broadcast_to(x, (1, 128))
    for copy in (u_copy, w0_copy, w1_copy, w2_copy):
        copy.wait()


def combine(coef, u, w0, w1, w2, psi):
    total = u[...].astype(f32) * coef[0, 0]
    total = total + w0[...].astype(f32) * coef[1, 0]
    total = total + w1[...].astype(f32) * coef[2, 0]
    psi[...] = total + w2[...].astype(f32) * coef[3, 0]


def on_device(peers, theta, env_left0, transfer, env_right, mpo_weights, term_mask, block_sizes, ritz):
    _, nsec, nstate, n, _ = theta.shape
    field = jax.ShapeDtypeStruct((nsec, nstate, n, n), bf16)
    small = jax.ShapeDtypeStruct((8, 128), f32)
    smem = pl.BlockSpec(memory_space=pltpu.SMEM)
    vmem = pl.BlockSpec(memory_space=pltpu.VMEM)
    hbm = pl.BlockSpec(memory_space=pl.ANY)
    dma = pltpu.SemaphoreType.DMA
    code = pltpu.VMEM((4, nsec, n + 16, n), jnp.int16)
    stack = pltpu.VMEM((nsec, nstate, n, n), bf16)
    u, w0, w1, w2, tri, coef = pl.pallas_call(
        kernel,
        out_shape=(field, field, field, field, small, small),
        in_specs=[smem, smem, smem, hbm, vmem, vmem, vmem, vmem],
        out_specs=(hbm, hbm, hbm, hbm, vmem, vmem),
        scratch_shapes=[
            code, code,
            pltpu.VMEM((nsec + 4, 2, n, n), bf16),
            pltpu.VMEM((2 * nstate * 16, nstate * 16), bf16),
            pltpu.VMEM((nsec, n, 2 * n), bf16),
            pltpu.VMEM((nsec, n, n), f32),
            stack, stack, stack, stack,
            pltpu.VMEM((nsec, 2, nstate, n, n), bf16),
            pltpu.VMEM((nsec, nstate, 2 * n, n), bf16),
            pltpu.VMEM((4, 4, 8, 128), f32),
            pltpu.VMEM((4, peers, 4, 8, 128), f32),
            dma, dma((4,)), dma((6,)), dma((6,)), dma((6,)), dma((6,)),
            dma((2,)), dma((2,)), dma((4, peers)), dma((4, peers)),
        ],
        compiler_params=pltpu.CompilerParams(
            collective_id=0, has_side_effects=True, vmem_limit_bytes=56 * 2**20
        ),
    )(
        block_sizes, term_mask, ritz, theta, env_left0, transfer, env_right,
        mpo_weights.reshape(2 * nstate, nstate),
    )
    span = 1024
    total = nsec * nstate * n
    flat = [x.reshape(total, n) for x in (u, w0, w1, w2)]
    block = pl.BlockSpec((span, n), lambda i: (i, 0))
    psi = pl.pallas_call(
        combine,
        grid=(total // span,),
        out_shape=jax.ShapeDtypeStruct((total, n), f32),
        in_specs=[smem] + [block] * 4,
        out_specs=block,
        compiler_params=pltpu.CompilerParams(vmem_limit_bytes=24 * 2**20),
    )(coef, *flat)
    return psi.reshape(theta.shape), tri[:6, 0].reshape(1, 2, 3)


def solution(mesh):
    in_specs = (
        P("chain", "sector", None, None, None),
        P("sector", None, None, None),
        P("chain", "sector", None, None),
        P("chain", "sector", None, None, None),
        P(),
        P("sector", None),
        P("sector"),
        P("chain", None),
    )
    out_specs = (P("chain", "sector", None, None, None), P("chain", None, None))
    return jax.shard_map(
        functools.partial(on_device, mesh.shape["sector"]),
        mesh=mesh, in_specs=in_specs, out_specs=out_specs, check_vma=False,
    )
```

```python
import functools

import jax
import jax.numpy as jnp
from jax import lax
from jax.experimental import pallas as pl
from jax.experimental.pallas import tpu as pltpu
from jax.sharding import PartitionSpec as P

f32, bf16 = jnp.float32, jnp.bfloat16
MESH = pl.DeviceIdType.MESH
group_bounds = [(0, 1), (1, 5), (5, 11), (11, 15), (15, 16)]
eps = 1e-6
LINE = 4
TOP = 32767.0


def split(x):
    high = x.astype(bf16)
    return high, (x - high.astype(f32)).astype(bf16)


def mm(a, b):
    return jnp.dot(a, b, preferred_element_type=f32)


def mm_nt(a, b):
    return lax.dot_general(a, b, (((1,), (1,)), ((), ())), preferred_element_type=f32)


def mm3(a, b):
    return mm(a[0], b[0]) + mm(a[0], b[1]) + mm(a[1], b[0])


def encode(x, ref):
    n = x.shape[0]
    top = jnp.max(jnp.abs(x), axis=0, keepdims=True)
    power = jnp.ceil(jnp.log2(jnp.maximum(top, 1e-35)) + 0.01)
    code = jnp.round(x * (jnp.exp2(-power) * TOP))
    ref[0:n] = code.astype(jnp.int32).astype(jnp.int16)
    ref[n : n + 16] = jnp.broadcast_to(power, (16, x.shape[1])).astype(jnp.int32).astype(jnp.int16)


def decode(ref):
    n = ref.shape[0] - 16
    power = ref[n : n + 16].astype(jnp.int32).astype(f32)[0:1]
    return ref[0:n].astype(jnp.int32).astype(f32) * (jnp.exp2(power) * (1.0 / TOP))


def fold(x):
    return jnp.sum(x.reshape(-1, 8, x.shape[-1]), axis=0)


def kernel(
    sizes, gates, ritz, theta, env_left, transfer, env_right, weights,
    u, w0, w1, w2, tri_out, coef_out,
    gbuf, tbuf, rbuf, wk, env, ypre, mixed, half, ex_src, ex_dst, factor, base_env,
    in_sem, g_send, g_recv, t_send, t_recv, r_send, r_recv, e_send, e_recv,
):
    nsec, nstate, n = u.shape[0], u.shape[1], u.shape[-1]
    chain, sector = lax.axis_index("chain"), lax.axis_index("sector")
    peers = ex_dst.shape[1]
    count = float(peers * nsec * nstate * n * n)
    z, y = chain // LINE, lax.rem(chain, LINE)

    def on_y(d):
        return (z * LINE + lax.rem(y + d, LINE), sector)

    def on_z(d):
        return (lax.rem(z + d, LINE) * LINE + y, sector)

    def on_sector(d):
        return (chain, lax.rem(sector + d, peers))

    barrier = pltpu.get_barrier_semaphore()
    others = [on_y(1), on_y(LINE - 1), on_z(1), on_z(LINE - 1)] + [on_sector(d) for d in range(1, peers)]
    for other in others:
        pl.semaphore_signal(barrier, inc=1, device_id=other, device_id_type=MESH)

    incoming = [
        pltpu.make_async_copy(src, dst, in_sem.at[i])
        for i, (src, dst) in enumerate((
            (transfer.at[0], factor), (env_right.at[0], rbuf.at[pl.ds(2, 2)]), (theta.at[0], u), (env_left, base_env),
        ))
    ]
    for copy in incoming:
        copy.start()
    rows = lax.broadcasted_iota(jnp.int32, (n, n), 0)
    cols = lax.broadcasted_iota(jnp.int32, (n, n), 1)

    def mask_of(s):
        return jnp.where((rows < sizes[s]) & (cols < sizes[s]), 1.0, 0.0).astype(f32)

    incoming[0].wait()
    for s in range(nsec):
        encode(factor[s] * mask_of(s), gbuf.at[0, s])
    pl.semaphore_wait(barrier, len(others))

    def remote(src, dst, send, recv, device):
        copy = pltpu.make_async_remote_copy(
            src_ref=src, dst_ref=dst, send_sem=send, recv_sem=recv,
            device_id=device, device_id_type=MESH,
        )
        copy.start()
        return copy

    pending = []
    upper, lower = pl.ds(0, n // 2), pl.ds(n // 2, n // 2 + 16)

    def line_send(buf, s, send, recv, onward, back):
        plan = ((1, upper, onward), (3, lower, back), (1, lower, onward), (3, upper, back))
        copies = [
            remote(buf.at[0, s, part], buf.at[place, s, part], send.at[s, i], recv.at[s, i], device)
            for i, (place, part, device) in enumerate(plan)
        ]
        pending.extend(copies)
        return copies

    def line_forward(copies, buf, s, send, recv, onward, back):
        for i, (place, part, device) in enumerate(((1, upper, onward), (3, lower, back))):
            copies[i].wait_recv()
            copy = remote(buf.at[place, s, part], buf.at[2, s, part], send.at[s, 4 + i], recv.at[s, 4 + i], device)
            copies.append(copy)
            pending.append(copy)

    def line_finish(copies):
        for copy in copies[2:]:
            copy.wait_recv()

    def exchange_start(e, sums):
        for i, x in enumerate(sums):
            ex_src[e, i] = x[:, :128] + x[:, 128:]
        for i in range(len(sums), ex_src.shape[1]):
            ex_src[e, i] = jnp.zeros((8, 128), f32)
        ex_dst[e, sector] = ex_src[e]
        copies = [
            remote(ex_src.at[e], ex_dst.at[e, sector], e_send.at[e, d], e_recv.at[e, d], on_sector(d))
            for d in range(1, peers)
        ]
        pending.extend(copies)
        return copies

    def exchange_finish(e, copies, amount):
        for copy in copies:
            copy.wait_recv()
        total = ex_dst[e, 0]
        for d in range(1, peers):
            total = total + ex_dst[e, d]
        return [jnp.sum(jnp.sum(total[i], axis=0, keepdims=True), axis=1, keepdims=True) for i in range(amount)]

    def mix(src, s):
        def step(i, _):
            span = pl.ds(pl.multiple_of(i * 16, 16), 16)
            block = src[s, :, span, :].reshape(nstate * 16, n)
            out = mm(wk[...], block).astype(bf16).reshape(2, nstate, 16, n)
            mixed[s, :, :, span, :] = out
            return 0

        lax.fori_loop(0, n // 16, step, 0, unroll=True)

    def right_side(s):
        for level, (begin, finish) in enumerate(group_bounds):
            for w in range(2):
                def step(p, _):
                    half[s, p, w * n : (w + 1) * n, :] = mm_nt(mixed[s, w, p], rbuf[s + level, w]).astype(bf16)
                    return 0

                lax.fori_loop(begin, finish, step, 0, unroll=True)

    def left_of(finish, s, accs):
        def on_state(p, accs):
            values = finish(s, p, mm(env[s], half[s, p]))
            return tuple(a + fold(v) for a, v in zip(accs, values))

        return lax.fori_loop(0, nstate, on_state, accs, unroll=True)

    def zeros(sums):
        return tuple(jnp.zeros((8, n), f32) for _ in range(sums))

    def left_side(finish, sums):
        return lax.fori_loop(0, nsec, lambda s, accs: left_of(finish, s, accs), zeros(sums))

    ring_y = (g_send, g_recv, on_y(1), on_y(LINE - 1))
    ring_z = (t_send, t_recv, on_z(1), on_z(LINE - 1))
    copies = [line_send(gbuf, s, *ring_y) for s in range(nsec)]
    incoming[1].wait()
    for s in range(nsec):
        mask = mask_of(s)
        for w in range(2):
            rbuf[2 + s, w] = (rbuf[2 + s, w].astype(f32) * mask).astype(bf16)
    halo = (
        remote(rbuf.at[pl.ds(2, 2)], rbuf.at[pl.ds(0, 2)], r_send.at[0], r_recv.at[0], on_sector(1)),
        remote(rbuf.at[pl.ds(2, 2)], rbuf.at[pl.ds(4, 2)], r_send.at[1], r_recv.at[1], on_sector(peers - 1)),
    )

    def charge(p):
        return sum((p >= bound).astype(jnp.int32) for bound in (1, 5, 11, 15))

    shape = (2 * nstate, nstate)
    state_row = lax.broadcasted_iota(jnp.int32, shape, 0) % nstate
    state_col = lax.broadcasted_iota(jnp.int32, shape, 1)
    table = jnp.where(charge(state_row) == charge(state_col), weights[...], 0.0).astype(bf16)
    tall = (2 * nstate * 16, 2 * nstate)
    spread_rows = jnp.where(
        lax.broadcasted_iota(jnp.int32, tall, 0) // 16 == lax.broadcasted_iota(jnp.int32, tall, 1), 1.0, 0.0
    ).astype(bf16)
    wide = (nstate, nstate * 16)
    spread_cols = jnp.where(
        lax.broadcasted_iota(jnp.int32, wide, 1) // 16 == lax.broadcasted_iota(jnp.int32, wide, 0), 1.0, 0.0
    ).astype(bf16)
    full = mm(mm(spread_rows, table).astype(bf16), spread_cols)
    big = full.shape
    same = lax.broadcasted_iota(jnp.int32, big, 0) % 16 == lax.broadcasted_iota(jnp.int32, big, 1) % 16
    wk[...] = jnp.where(same, full, 0.0).astype(bf16)

    incoming[2].wait()

    def masked(s, acc):
        mask = mask_of(s)

        def step(p, acc):
            value = u[s, p].astype(f32) * mask
            u[s, p] = value.astype(bf16)
            return acc + fold(value * value)

        return lax.fori_loop(0, nstate, step, acc, unroll=2)

    square = lax.fori_loop(0, nsec, masked, jnp.zeros((8, n), f32))
    started = exchange_start(0, [square])
    for s in range(nsec):
        line_forward(copies[s], gbuf, s, *ring_y)
        mix(u, s)

    def slot(buf, at, j, s):
        return decode(buf.at[lax.rem(at - j + LINE, LINE), s])

    for s in range(nsec):
        line_finish(copies[s])
        factors = [split(slot(gbuf, y, j, s)) for j in range(LINE)]
        second = mm3(factors[0], factors[1])
        later = mm3(factors[2], factors[3])
        ypre[s] = second
        encode(mm3(split(second), split(later)), tbuf.at[0, s])
        copies[s] = line_send(tbuf, s, *ring_z)

    eye = jnp.where(rows == cols, 1.0, 0.0).astype(f32)

    def chosen(at, values):
        return jnp.where(
            at == 0, eye, jnp.where(at == 1, values[0], jnp.where(at == 2, values[1], values[2]))
        )

    for s in range(nsec):
        second = ypre[s]
        third = mm3(split(second), split(slot(gbuf, y, 2, s)))
        ypre[s] = chosen(y, (slot(gbuf, y, 0, s), second, third))
    for copy in halo:
        copy.wait_recv()
    pending.extend(halo)

    @pl.when(sector == 0)
    def _():
        rbuf[0:2] = jnp.zeros_like(rbuf[0:2])

    @pl.when(sector == peers - 1)
    def _():
        rbuf[4:6] = jnp.zeros_like(rbuf[4:6])

    incoming[3].wait()
    (uu,) = exchange_finish(0, started, 1)
    for s in range(nsec):
        right_side(s)
        line_forward(copies[s], tbuf, s, *ring_z)

    inv_count = 1.0 / count

    def row(x):
        return jnp.broadcast_to(x, (1, n))

    c0 = 1.0 / jnp.sqrt(uu * inv_count + eps)
    k_c0 = row(c0)

    def finish0(s, p, image):
        value = image * k_c0
        w0[s, p] = value.astype(bf16)
        return value * u[s, p].astype(f32), value * value

    sums = zeros(2)
    for s in range(nsec):
        line_finish(copies[s])
        near = [jnp.where(z > j, slot(tbuf, z, j, s), eye) for j in range(LINE - 1)]
        front = mm3(split(near[0]), split(near[1]))
        back = mm3(split(near[2]), split(ypre[s]))
        prefix = mm3(split(front), split(back))
        high, low = split(prefix)
        high_t, low_t = split(prefix.T)
        mask = mask_of(s)
        for w in range(2):
            base = (base_env[s, w].astype(f32) * mask).astype(bf16)
            inner = split(mm(base, high) + mm(base, low))
            left = mm3((high_t, low_t), inner).astype(bf16).astype(f32) * gates[s, w].astype(f32)
            env[s, :, w * n : (w + 1) * n] = left.astype(bf16)
        sums = left_of(finish0, s, sums)
    started = exchange_start(1, sums)
    mix(w0, 0)
    right_side(0)
    mix(w0, 1)
    s1, s2 = exchange_finish(1, started, 2)

    def inverse(x):
        return 1.0 / x

    def root(x):
        return jnp.sqrt(jnp.maximum(x, 0.0) * inv_count + eps)

    n00 = c0 * c0 * uu
    v0w0 = c0 * s1
    a0 = v0w0 * inv_count
    r0 = s2 - 2.0 * a0 * v0w0 + a0 * a0 * n00
    b0 = root(r0)
    i0 = inverse(b0)
    n11 = r0 * i0 * i0
    n01 = (v0w0 - a0 * n00) * i0

    k_image, k_w0 = row(i0), row(a0 * i0)
    right_side(1)

    def finish1(s, p, image):
        before = w0[s, p].astype(f32)
        value = image * k_image - before * k_w0
        w1[s, p] = value.astype(bf16)
        return value * u[s, p].astype(f32), value * before, value * value

    started = exchange_start(2, left_side(finish1, 3))
    mix(w1, 0)
    right_side(0)
    mix(w1, 1)
    d0, d1, d2 = exchange_finish(2, started, 3)
    v0w1 = c0 * d0
    v1w1 = (d1 - a0 * v0w1) * i0
    a1 = v1w1 * inv_count
    r1 = d2 + a1 * a1 * n11 + b0 * b0 * n00 - 2.0 * a1 * v1w1 - 2.0 * b0 * v0w1 + 2.0 * a1 * b0 * n01
    b1 = root(r1)
    i1 = inverse(b1)
    n22 = r1 * i1 * i1
    n12 = (v1w1 - a1 * n11 - b0 * n01) * i1

    k_image2, k_w1, k_w02 = row(i1), row(a1 * i1), row(b0 * i1)
    right_side(1)

    def finish2(s, p, image):
        older, before = w0[s, p].astype(f32), w1[s, p].astype(f32)
        value = image * k_image2 - before * k_w1 - older * k_w02
        w2[s, p] = value.astype(bf16)
        return value * u[s, p].astype(f32), value * older, value * before, value * value

    started = exchange_start(3, left_side(finish2, 4))
    f0, f1, f2, f3 = exchange_finish(3, started, 4)
    v0w2 = c0 * f0
    v1w2 = (f1 - a0 * v0w2) * i0
    v2w2 = (f2 - a1 * v1w2 - b0 * v0w2) * i1
    a2 = v2w2 * inv_count
    r2 = f3 + a2 * a2 * n22 + b1 * b1 * n11 - 2.0 * a2 * v2w2 - 2.0 * b1 * v1w2 + 2.0 * a2 * b1 * n12
    b2 = root(r2)
    k3 = ritz[0, 3] / b2
    m2 = ritz[0, 2] - k3 * a2
    m1 = ritz[0, 1] - k3 * b1 - m2 * a1 * i1
    m0 = ritz[0, 0] - m2 * b0 * i1 - m1 * a0 * i0
    lane = lax.broadcasted_iota(jnp.int32, (1, 128), 1)
    for i, (x, y0, y1) in enumerate(((a0, a1, a2), (b0, b1, b2))):
        tri_out[i : i + 1, :] = jnp.where(lane == 0, x, jnp.where(lane == 1, y0, y1))
    for i, x in enumerate((m0 * c0, m1 * i0, m2 * i1, k3)):
        coef_out[i : i + 1, :] = row(x)
    for copy in pending:
        copy.wait_send()


def combine(coef, tri, u, w0, w1, w2, psi, tri_out, block, sems):
    tri_out[0] = tri[0:2, 0:3]
    parts = sems.shape[0]
    span = u.shape[0] // parts
    weights = [coef[i : i + 1, :] for i in range(4)]
    copies = []
    for part in range(parts):
        rows = pl.ds(part * span, span)

        def step(i, _):
            some = pl.ds(pl.multiple_of(part * span + i * 64, 64), 64)
            total = u[some, :].astype(f32) * weights[0]
            total = total + w0[some, :].astype(f32) * weights[1]
            total = total + w1[some, :].astype(f32) * weights[2]
            block[some, :] = total + w2[some, :].astype(f32) * weights[3]
            return 0

        lax.fori_loop(0, span // 64, step, 0, unroll=4)
        copy = pltpu.make_async_copy(block.at[rows], psi.at[rows], sems.at[part])
        copy.start()
        copies.append(copy)
    for copy in copies:
        copy.wait()


def on_device(peers, theta, env_left0, transfer, env_right, mpo_weights, term_mask, block_sizes, ritz):
    _, nsec, nstate, n, _ = theta.shape
    field = pltpu.VMEM((nsec, nstate, n, n), bf16)
    smem = pl.BlockSpec(memory_space=pltpu.SMEM)
    vmem = pl.BlockSpec(memory_space=pltpu.VMEM)
    hbm = pl.BlockSpec(memory_space=pl.ANY)
    dma = pltpu.SemaphoreType.DMA
    code = pltpu.VMEM((4, nsec, n + 16, n), jnp.int16)
    u, w0, w1, w2, tri, coef = pl.pallas_call(
        kernel,
        out_shape=(field, field, field, field, pltpu.VMEM((8, 128), f32), pltpu.VMEM((8, n), f32)),
        in_specs=[smem, smem, smem, hbm, hbm, hbm, hbm, vmem],
        out_specs=(vmem,) * 6,
        scratch_shapes=[
            code, code,
            pltpu.VMEM((nsec + 4, 2, n, n), bf16),
            pltpu.VMEM((2 * nstate * 16, nstate * 16), bf16),
            pltpu.VMEM((nsec, n, 2 * n), bf16),
            pltpu.VMEM((nsec, n, n), f32),
            pltpu.VMEM((nsec, 2, nstate, n, n), bf16),
            pltpu.VMEM((nsec, nstate, 2 * n, n), bf16),
            pltpu.VMEM((4, 4, 8, 128), f32),
            pltpu.VMEM((4, peers, 4, 8, 128), f32),
            pltpu.VMEM((nsec, n, n), f32),
            pltpu.VMEM((nsec, 2, n, n), bf16),
            dma((4,)), dma((nsec, 6)), dma((nsec, 6)), dma((nsec, 6)), dma((nsec, 6)),
            dma((2,)), dma((2,)), dma((4, peers)), dma((4, peers)),
        ],
        compiler_params=pltpu.CompilerParams(
            collective_id=0, has_side_effects=True, vmem_limit_bytes=40 * 2**20
        ),
    )(
        block_sizes, term_mask, ritz, theta, env_left0, transfer, env_right,
        mpo_weights.reshape(2 * nstate, nstate),
    )
    total = nsec * nstate * n
    flat = [x.reshape(total, n) for x in (u, w0, w1, w2)]
    parts = 16
    psi, tridiag = pl.pallas_call(
        combine,
        out_shape=(jax.ShapeDtypeStruct((total, n), f32), jax.ShapeDtypeStruct((1, 2, 3), f32)),
        in_specs=[vmem] * 6,
        out_specs=(hbm, vmem),
        scratch_shapes=[pltpu.VMEM((total, n), f32), dma((parts,))],
        compiler_params=pltpu.CompilerParams(vmem_limit_bytes=24 * 2**20),
    )(coef, tri, *flat)
    return psi.reshape(theta.shape), tridiag


def solution(mesh):
    in_specs = (
        P("chain", "sector", None, None, None),
        P("sector", None, None, None),
        P("chain", "sector", None, None),
        P("chain", "sector", None, None, None),
        P(),
        P("sector", None),
        P("sector"),
        P("chain", None),
    )
    out_specs = (P("chain", "sector", None, None, None), P("chain", None, None))
    return jax.shard_map(
        functools.partial(on_device, mesh.shape["sector"]),
        mesh=mesh, in_specs=in_specs, out_specs=out_specs, check_vma=False,
    )
```

```python
import functools

import jax
import jax.numpy as jnp
from jax import lax
from jax.experimental import pallas as pl
from jax.experimental.pallas import tpu as pltpu
from jax.sharding import PartitionSpec as P

f32, bf16 = jnp.float32, jnp.bfloat16
MESH = pl.DeviceIdType.MESH
group_bounds = [(0, 1), (1, 5), (5, 11), (11, 15), (15, 16)]
eps = 1e-6
LINE = 4
TOP = 32767.0


def split(x):
    high = x.astype(bf16)
    return high, (x - high.astype(f32)).astype(bf16)


def mm(a, b):
    return jnp.dot(a, b, preferred_element_type=f32)


def mm_nt(a, b):
    return lax.dot_general(a, b, (((1,), (1,)), ((), ())), preferred_element_type=f32)


def mm3(a, b):
    return mm(a[0], b[0]) + mm(a[0], b[1]) + mm(a[1], b[0])


def encode(x, ref):
    n = x.shape[0]
    top = jnp.max(jnp.abs(x), axis=0, keepdims=True)
    power = jnp.ceil(jnp.log2(jnp.maximum(top, 1e-35)) + 0.01)
    code = jnp.round(x * (jnp.exp2(-power) * TOP))
    ref[0:n] = code.astype(jnp.int32).astype(jnp.int16)
    ref[n : n + 16] = jnp.broadcast_to(power, (16, x.shape[1])).astype(jnp.int32).astype(jnp.int16)


def decode(ref):
    n = ref.shape[0] - 16
    power = ref[n : n + 16].astype(jnp.int32).astype(f32)[0:1]
    return ref[0:n].astype(jnp.int32).astype(f32) * (jnp.exp2(power) * (1.0 / TOP))


def fold(x):
    return jnp.sum(x.reshape(-1, 8, x.shape[-1]), axis=0)


def kernel(
    sizes, gates, ritz, theta, env_left, transfer, env_right, weights,
    u, w0, w1, w2, tri_out, coef_out,
    gbuf, tbuf, rbuf, wk, env, ypre, mixed, half, ex_src, ex_dst, factor, base_env,
    in_sem, g_send, g_recv, t_send, t_recv, r_send, r_recv, e_send, e_recv,
):
    nsec, nstate, n = u.shape[0], u.shape[1], u.shape[-1]
    chain, sector = lax.axis_index("chain"), lax.axis_index("sector")
    peers = ex_dst.shape[1]
    count = float(peers * nsec * nstate * n * n)
    z, y = chain // LINE, lax.rem(chain, LINE)

    def on_y(d):
        return (z * LINE + lax.rem(y + d, LINE), sector)

    def on_z(d):
        return (lax.rem(z + d, LINE) * LINE + y, sector)

    def on_sector(d):
        return (chain, lax.rem(sector + d, peers))

    barrier = pltpu.get_barrier_semaphore()
    others = [on_y(1), on_y(LINE - 1), on_z(1), on_z(LINE - 1)] + [on_sector(d) for d in range(1, peers)]
    for other in others:
        pl.semaphore_signal(barrier, inc=1, device_id=other, device_id_type=MESH)

    incoming = [
        pltpu.make_async_copy(src, dst, in_sem.at[i])
        for i, (src, dst) in enumerate((
            (transfer.at[0], factor), (env_right.at[0], rbuf.at[pl.ds(2, 2)]), (theta.at[0], u), (env_left, base_env),
        ))
    ]
    for copy in incoming:
        copy.start()
    rows = lax.broadcasted_iota(jnp.int32, (n, n), 0)
    cols = lax.broadcasted_iota(jnp.int32, (n, n), 1)

    def mask_of(s):
        return jnp.where((rows < sizes[s]) & (cols < sizes[s]), 1.0, 0.0).astype(f32)

    incoming[0].wait()
    for s in range(nsec):
        encode(factor[s] * mask_of(s), gbuf.at[0, s])
    pl.semaphore_wait(barrier, len(others))

    def remote(src, dst, send, recv, device):
        copy = pltpu.make_async_remote_copy(
            src_ref=src, dst_ref=dst, send_sem=send, recv_sem=recv,
            device_id=device, device_id_type=MESH,
        )
        copy.start()
        return copy

    pending = []
    upper, lower = pl.ds(0, n // 2), pl.ds(n // 2, n // 2 + 16)

    def line_send(buf, s, send, recv, onward, back):
        plan = ((1, upper, onward), (3, lower, back), (1, lower, onward), (3, upper, back))
        copies = [
            remote(buf.at[0, s, part], buf.at[place, s, part], send.at[s, i], recv.at[s, i], device)
            for i, (place, part, device) in enumerate(plan)
        ]
        pending.extend(copies)
        return copies

    def line_forward(copies, buf, s, send, recv, onward, back):
        for i, (place, part, device) in enumerate(((1, upper, onward), (3, lower, back))):
            copies[i].wait_recv()
            copy = remote(buf.at[place, s, part], buf.at[2, s, part], send.at[s, 4 + i], recv.at[s, 4 + i], device)
            copies.append(copy)
            pending.append(copy)

    def line_finish(copies):
        for copy in copies[2:]:
            copy.wait_recv()

    def exchange_start(e, sums):
        place = lax.broadcasted_iota(jnp.int32, (8, 128), 0)
        tile = jnp.zeros((8, 128), f32)
        for i, x in enumerate(sums):
            tile = jnp.where(place == i, jnp.sum(x[:, :128] + x[:, 128:], axis=0, keepdims=True), tile)
        ex_src[e] = tile
        copies = [
            remote(ex_src.at[e], ex_dst.at[e, sector], e_send.at[e, d], e_recv.at[e, d], on_sector(d))
            for d in range(1, peers)
        ]
        ex_dst[e, sector] = tile
        pending.extend(copies)
        return copies

    def exchange_finish(e, copies, amount):
        for copy in copies:
            copy.wait_recv()
        total = ex_dst[e, 0]
        for d in range(1, peers):
            total = total + ex_dst[e, d]
        sums = jnp.sum(total, axis=1, keepdims=True)
        return [sums[i : i + 1] for i in range(amount)]

    def mix(src, s):
        def step(i, _):
            span = pl.ds(pl.multiple_of(i * 16, 16), 16)
            block = src[s, :, span, :].reshape(nstate * 16, n)
            out = mm(wk[...], block).astype(bf16).reshape(2, nstate, 16, n)
            mixed[s, :, :, span, :] = out
            return 0

        lax.fori_loop(0, n // 16, step, 0, unroll=True)

    def right_side(s, levels=range(5)):
        for level in levels:
            begin, finish = group_bounds[level]
            for w in range(2):
                def step(p, _):
                    half[s, p, w * n : (w + 1) * n, :] = mm_nt(mixed[s, w, p], rbuf[s + level, w]).astype(bf16)
                    return 0

                lax.fori_loop(begin, finish, step, 0, unroll=True)

    def left_of(finish, s, accs):
        def on_state(p, accs):
            values = finish(s, p, mm(env[s], half[s, p]))
            return tuple(a + fold(v) for a, v in zip(accs, values))

        return lax.fori_loop(0, nstate, on_state, accs, unroll=True)

    def zeros(sums):
        return tuple(jnp.zeros((8, n), f32) for _ in range(sums))

    def left_side(finish, sums):
        return lax.fori_loop(0, nsec, lambda s, accs: left_of(finish, s, accs), zeros(sums))

    ring_y = (g_send, g_recv, on_y(1), on_y(LINE - 1))
    ring_z = (t_send, t_recv, on_z(1), on_z(LINE - 1))
    copies = [line_send(gbuf, s, *ring_y) for s in range(nsec)]
    incoming[1].wait()
    for s in range(nsec):
        mask = mask_of(s)
        for w in range(2):
            rbuf[2 + s, w] = (rbuf[2 + s, w].astype(f32) * mask).astype(bf16)
    halo = (
        remote(rbuf.at[pl.ds(2, 2)], rbuf.at[pl.ds(0, 2)], r_send.at[0], r_recv.at[0], on_sector(1)),
        remote(rbuf.at[pl.ds(2, 2)], rbuf.at[pl.ds(4, 2)], r_send.at[1], r_recv.at[1], on_sector(peers - 1)),
    )

    def charge(p):
        return sum((p >= bound).astype(jnp.int32) for bound in (1, 5, 11, 15))

    shape = (2 * nstate, nstate)
    state_row = lax.broadcasted_iota(jnp.int32, shape, 0) % nstate
    state_col = lax.broadcasted_iota(jnp.int32, shape, 1)
    table = jnp.where(charge(state_row) == charge(state_col), weights[...], 0.0).astype(bf16)
    tall = (2 * nstate * 16, 2 * nstate)
    spread_rows = jnp.where(
        lax.broadcasted_iota(jnp.int32, tall, 0) // 16 == lax.broadcasted_iota(jnp.int32, tall, 1), 1.0, 0.0
    ).astype(bf16)
    wide = (nstate, nstate * 16)
    spread_cols = jnp.where(
        lax.broadcasted_iota(jnp.int32, wide, 1) // 16 == lax.broadcasted_iota(jnp.int32, wide, 0), 1.0, 0.0
    ).astype(bf16)
    full = mm(mm(spread_rows, table).astype(bf16), spread_cols)
    big = full.shape
    same = lax.broadcasted_iota(jnp.int32, big, 0) % 16 == lax.broadcasted_iota(jnp.int32, big, 1) % 16
    wk[...] = jnp.where(same, full, 0.0).astype(bf16)

    incoming[2].wait()

    def masked(s, acc):
        mask = mask_of(s)

        def step(p, acc):
            value = u[s, p].astype(f32) * mask
            u[s, p] = value.astype(bf16)
            return acc + fold(value * value)

        return lax.fori_loop(0, nstate, step, acc, unroll=2)

    square = lax.fori_loop(0, nsec, masked, jnp.zeros((8, n), f32))
    started = exchange_start(0, [square])
    for s in range(nsec):
        line_forward(copies[s], gbuf, s, *ring_y)
        mix(u, s)

    def slot(buf, at, j, s):
        return decode(buf.at[lax.rem(at - j + LINE, LINE), s])

    for s in range(nsec):
        line_finish(copies[s])
        factors = [split(slot(gbuf, y, j, s)) for j in range(LINE)]
        second = mm3(factors[0], factors[1])
        later = mm3(factors[2], factors[3])
        ypre[s] = second
        encode(mm3(split(second), split(later)), tbuf.at[0, s])
        copies[s] = line_send(tbuf, s, *ring_z)

    eye = jnp.where(rows == cols, 1.0, 0.0).astype(f32)

    def chosen(at, values):
        return jnp.where(
            at == 0, eye, jnp.where(at == 1, values[0], jnp.where(at == 2, values[1], values[2]))
        )

    for s in range(nsec):
        second = ypre[s]
        third = mm3(split(second), split(slot(gbuf, y, 2, s)))
        ypre[s] = chosen(y, (slot(gbuf, y, 0, s), second, third))
    for copy in halo:
        copy.wait_recv()
    pending.extend(halo)

    @pl.when(sector == 0)
    def _():
        rbuf[0:2] = jnp.zeros_like(rbuf[0:2])

    @pl.when(sector == peers - 1)
    def _():
        rbuf[4:6] = jnp.zeros_like(rbuf[4:6])

    incoming[3].wait()
    (uu,) = exchange_finish(0, started, 1)
    for s in range(nsec):
        right_side(s)
        line_forward(copies[s], tbuf, s, *ring_z)

    inv_count = 1.0 / count

    def row(x):
        return jnp.broadcast_to(x, (1, n))

    c0 = 1.0 / jnp.sqrt(uu * inv_count + eps)
    k_c0 = row(c0)

    def finish0(s, p, image):
        value = image * k_c0
        w0[s, p] = value.astype(bf16)
        return value * u[s, p].astype(f32), value * value

    sums = zeros(2)
    for s in range(nsec):
        line_finish(copies[s])
        near = [jnp.where(z > j, slot(tbuf, z, j, s), eye) for j in range(LINE - 1)]
        front = mm3(split(near[0]), split(near[1]))
        back = mm3(split(near[2]), split(ypre[s]))
        prefix = mm3(split(front), split(back))
        high, low = split(prefix)
        high_t, low_t = split(prefix.T)
        mask = mask_of(s)
        for w in range(2):
            base = (base_env[s, w].astype(f32) * mask).astype(bf16)
            inner = split(mm(base, high) + mm(base, low))
            left = mm3((high_t, low_t), inner).astype(bf16).astype(f32) * gates[s, w].astype(f32)
            env[s, :, w * n : (w + 1) * n] = left.astype(bf16)
        sums = left_of(finish0, s, sums)
    started = exchange_start(1, sums)
    mix(w0, 0)
    right_side(0)
    mix(w0, 1)
    right_side(1, range(3))
    s1, s2 = exchange_finish(1, started, 2)

    def inverse(x):
        return 1.0 / x

    def root(x):
        return jnp.sqrt(jnp.maximum(x, 0.0) * inv_count + eps)

    n00 = c0 * c0 * uu
    v0w0 = c0 * s1
    a0 = v0w0 * inv_count
    r0 = s2 - 2.0 * a0 * v0w0 + a0 * a0 * n00
    b0 = root(r0)
    i0 = inverse(b0)
    n11 = r0 * i0 * i0
    n01 = (v0w0 - a0 * n00) * i0

    k_image, k_w0 = row(i0 * i0), row(a0 * i0 * i0)
    right_side(1, range(3, 5))

    def finish1(s, p, image):
        before = w0[s, p].astype(f32)
        value = image * k_image - before * k_w0
        w1[s, p] = value.astype(bf16)
        return value * u[s, p].astype(f32), value * before, value * value

    started = exchange_start(2, left_side(finish1, 3))
    for s in range(nsec):
        mix(w1, s)
        right_side(s)

    def finish2(s, p, image):
        w2[s, p] = image.astype(bf16)
        older, before = w0[s, p].astype(f32), w1[s, p].astype(f32)
        return image * u[s, p].astype(f32), image * older, image * before, image * image

    last = exchange_start(3, left_side(finish2, 4))
    d0, d1, d2 = exchange_finish(2, started, 3)
    v0w1 = c0 * d0 * b0
    v1w1 = d1 - a0 * c0 * d0
    w1w1 = d2 * b0 * b0
    a1 = v1w1 * inv_count
    r1 = w1w1 + a1 * a1 * n11 + b0 * b0 * n00 - 2.0 * a1 * v1w1 - 2.0 * b0 * v0w1 + 2.0 * a1 * b0 * n01
    b1 = root(r1)
    i1 = inverse(b1)
    n22 = r1 * i1 * i1
    n12 = (v1w1 - a1 * n11 - b0 * n01) * i1
    ratio = b0 * i1
    f0, f1, f2, f3 = exchange_finish(3, last, 4)
    v0w2 = c0 * ratio * (f0 - a1 * d0 - s1)
    v1w2 = (ratio * (f1 - a1 * d1 - s2) - a0 * v0w2) * i0
    w1w2 = b0 * ratio * (f2 - a1 * d2 - d1)
    w2w2 = ratio * ratio * (f3 + a1 * a1 * d2 + s2 - 2.0 * a1 * f2 - 2.0 * f1 + 2.0 * a1 * d1)
    v2w2 = (w1w2 - a1 * v1w2 - b0 * v0w2) * i1
    a2 = v2w2 * inv_count
    r2 = w2w2 + a2 * a2 * n22 + b1 * b1 * n11 - 2.0 * a2 * v2w2 - 2.0 * b1 * v1w2 + 2.0 * a2 * b1 * n12
    b2 = root(r2)
    k3 = ritz[0, 3] / b2
    m2 = ritz[0, 2] - k3 * a2
    m1 = ritz[0, 1] - k3 * b1 - m2 * a1 * i1
    m0 = ritz[0, 0] - m2 * b0 * i1 - m1 * a0 * i0
    k_last = k3 * ratio
    lane = lax.broadcasted_iota(jnp.int32, (1, 128), 1)
    for i, (x, y0, y1) in enumerate(((a0, a1, a2), (b0, b1, b2))):
        tri_out[i : i + 1, :] = jnp.where(lane == 0, x, jnp.where(lane == 1, y0, y1))
    for i, x in enumerate((m0 * c0, m1 * i0 - k_last, m2 * ratio - k_last * a1, k_last)):
        coef_out[i : i + 1, :] = row(x)
    for copy in pending:
        copy.wait_send()


def combine(coef, tri, u, w0, w1, w2, psi, tri_out, block, sems):
    tri_out[0] = tri[0:2, 0:3]
    parts = sems.shape[0]
    span = u.shape[0] // parts
    weights = [coef[i : i + 1, :] for i in range(4)]
    copies = []
    for part in range(parts):
        rows = pl.ds(part * span, span)

        def step(i, _):
            some = pl.ds(pl.multiple_of(part * span + i * 64, 64), 64)
            total = u[some, :].astype(f32) * weights[0]
            total = total + w0[some, :].astype(f32) * weights[1]
            total = total + w1[some, :].astype(f32) * weights[2]
            block[some, :] = total + w2[some, :].astype(f32) * weights[3]
            return 0

        lax.fori_loop(0, span // 64, step, 0, unroll=4)
        copy = pltpu.make_async_copy(block.at[rows], psi.at[rows], sems.at[part])
        copy.start()
        copies.append(copy)
    for copy in copies:
        copy.wait()


def on_device(peers, theta, env_left0, transfer, env_right, mpo_weights, term_mask, block_sizes, ritz):
    _, nsec, nstate, n, _ = theta.shape
    field = pltpu.VMEM((nsec, nstate, n, n), bf16)
    smem = pl.BlockSpec(memory_space=pltpu.SMEM)
    vmem = pl.BlockSpec(memory_space=pltpu.VMEM)
    hbm = pl.BlockSpec(memory_space=pl.ANY)
    dma = pltpu.SemaphoreType.DMA
    code = pltpu.VMEM((4, nsec, n + 16, n), jnp.int16)
    u, w0, w1, w2, tri, coef = pl.pallas_call(
        kernel,
        out_shape=(field, field, field, field, pltpu.VMEM((8, 128), f32), pltpu.VMEM((8, n), f32)),
        in_specs=[smem, smem, smem, hbm, hbm, hbm, hbm, vmem],
        out_specs=(vmem,) * 6,
        scratch_shapes=[
            code, code,
            pltpu.VMEM((nsec + 4, 2, n, n), bf16),
            pltpu.VMEM((2 * nstate * 16, nstate * 16), bf16),
            pltpu.VMEM((nsec, n, 2 * n), bf16),
            pltpu.VMEM((nsec, n, n), f32),
            pltpu.VMEM((nsec, 2, nstate, n, n), bf16),
            pltpu.VMEM((nsec, nstate, 2 * n, n), bf16),
            pltpu.VMEM((4, 8, 128), f32),
            pltpu.VMEM((4, peers, 8, 128), f32),
            pltpu.VMEM((nsec, n, n), f32),
            pltpu.VMEM((nsec, 2, n, n), bf16),
            dma((4,)), dma((nsec, 6)), dma((nsec, 6)), dma((nsec, 6)), dma((nsec, 6)),
            dma((2,)), dma((2,)), dma((4, peers)), dma((4, peers)),
        ],
        compiler_params=pltpu.CompilerParams(
            collective_id=0, has_side_effects=True, vmem_limit_bytes=40 * 2**20
        ),
    )(
        block_sizes, term_mask, ritz, theta, env_left0, transfer, env_right,
        mpo_weights.reshape(2 * nstate, nstate),
    )
    total = nsec * nstate * n
    flat = [x.reshape(total, n) for x in (u, w0, w1, w2)]
    parts = 16
    psi, tridiag = pl.pallas_call(
        combine,
        out_shape=(jax.ShapeDtypeStruct((total, n), f32), jax.ShapeDtypeStruct((1, 2, 3), f32)),
        in_specs=[vmem] * 6,
        out_specs=(hbm, vmem),
        scratch_shapes=[pltpu.VMEM((total, n), f32), dma((parts,))],
        compiler_params=pltpu.CompilerParams(vmem_limit_bytes=24 * 2**20),
    )(coef, tri, *flat)
    return psi.reshape(theta.shape), tridiag


def solution(mesh):
    in_specs = (
        P("chain", "sector", None, None, None),
        P("sector", None, None, None),
        P("chain", "sector", None, None),
        P("chain", "sector", None, None, None),
        P(),
        P("sector", None),
        P("sector"),
        P("chain", None),
    )
    out_specs = (P("chain", "sector", None, None, None), P("chain", None, None))
    return jax.shard_map(
        functools.partial(on_device, mesh.shape["sector"]),
        mesh=mesh, in_specs=in_specs, out_specs=out_specs, check_vma=False,
    )
```

```python
import functools

import jax
import jax.numpy as jnp
from jax import lax
from jax.experimental import pallas as pl
from jax.experimental.pallas import tpu as pltpu
from jax.sharding import PartitionSpec as P

f32, bf16 = jnp.float32, jnp.bfloat16
MESH = pl.DeviceIdType.MESH
group_bounds = [(0, 1), (1, 5), (5, 11), (11, 15), (15, 16)]
eps = 1e-6
LINE = 4
TOP = 32767.0


def split(x):
    high = x.astype(bf16)
    return high, (x - high.astype(f32)).astype(bf16)


def mm(a, b):
    return jnp.dot(a, b, preferred_element_type=f32)


def mm_nt(a, b):
    return lax.dot_general(a, b, (((1,), (1,)), ((), ())), preferred_element_type=f32)


def mm3(a, b):
    return mm(a[0], b[0]) + mm(a[0], b[1]) + mm(a[1], b[0])


def encode(x, ref):
    n = x.shape[0]
    top = jnp.max(jnp.abs(x), axis=0, keepdims=True)
    power = jnp.ceil(jnp.log2(jnp.maximum(top, 1e-35)) + 0.01)
    code = jnp.round(x * (jnp.exp2(-power) * TOP))
    ref[0:n] = code.astype(jnp.int32).astype(jnp.int16)
    ref[n : n + 16] = jnp.broadcast_to(power, (16, x.shape[1])).astype(jnp.int32).astype(jnp.int16)


def decode(ref):
    n = ref.shape[0] - 16
    power = ref[n : n + 16].astype(jnp.int32).astype(f32)[0:1]
    return ref[0:n].astype(jnp.int32).astype(f32) * (jnp.exp2(power) * (1.0 / TOP))


def fold(x):
    return jnp.sum(x.reshape(-1, 8, x.shape[-1]), axis=0)


def kernel(
    sizes, gates, ritz, theta, env_left, transfer, env_right, weights,
    u, w0, w1, w2, tri_out, coef_out,
    gbuf, tbuf, rbuf, wk, env, ypre, mixed, half, ex_src, ex_dst, factor, base_env,
    in_sem, g_send, g_recv, t_send, t_recv, r_send, r_recv, e_send, e_recv,
):
    nsec, nstate, n = u.shape[0], u.shape[1], u.shape[-1]
    chain, sector = lax.axis_index("chain"), lax.axis_index("sector")
    peers = ex_dst.shape[1]
    count = float(peers * nsec * nstate * n * n)
    z, y = chain // LINE, lax.rem(chain, LINE)

    def on_y(d):
        return (z * LINE + lax.rem(y + d, LINE), sector)

    def on_z(d):
        return (lax.rem(z + d, LINE) * LINE + y, sector)

    def on_sector(d):
        return (chain, lax.rem(sector + d, peers))

    barrier = pltpu.get_barrier_semaphore()
    others = [on_y(1), on_y(LINE - 1), on_z(1), on_z(LINE - 1)] + [on_sector(d) for d in range(1, peers)]
    for other in others:
        pl.semaphore_signal(barrier, inc=1, device_id=other, device_id_type=MESH)

    incoming = [
        pltpu.make_async_copy(src, dst, in_sem.at[i])
        for i, (src, dst) in enumerate((
            (transfer.at[0], factor), (env_right.at[0], rbuf.at[pl.ds(2, 2)]), (theta.at[0], u), (env_left, base_env),
        ))
    ]
    for copy in incoming:
        copy.start()
    rows = lax.broadcasted_iota(jnp.int32, (n, n), 0)
    cols = lax.broadcasted_iota(jnp.int32, (n, n), 1)

    def mask_of(s):
        return jnp.where((rows < sizes[s]) & (cols < sizes[s]), 1.0, 0.0).astype(f32)

    incoming[0].wait()
    for s in range(nsec):
        encode(factor[s] * mask_of(s), gbuf.at[0, s])
    pl.semaphore_wait(barrier, len(others))

    def remote(src, dst, send, recv, device):
        copy = pltpu.make_async_remote_copy(
            src_ref=src, dst_ref=dst, send_sem=send, recv_sem=recv,
            device_id=device, device_id_type=MESH,
        )
        copy.start()
        return copy

    pending = []
    upper, lower = pl.ds(0, n // 2), pl.ds(n // 2, n // 2 + 16)

    def line_send(buf, s, send, recv, onward, back):
        plan = ((1, upper, onward), (3, lower, back), (1, lower, onward), (3, upper, back))
        copies = [
            remote(buf.at[0, s, part], buf.at[place, s, part], send.at[s, i], recv.at[s, i], device)
            for i, (place, part, device) in enumerate(plan)
        ]
        pending.extend(copies)
        return copies

    def line_forward(copies, buf, s, send, recv, onward, back):
        for i, (place, part, device) in enumerate(((1, upper, onward), (3, lower, back))):
            copies[i].wait_recv()
            copy = remote(buf.at[place, s, part], buf.at[2, s, part], send.at[s, 4 + i], recv.at[s, 4 + i], device)
            copies.append(copy)
            pending.append(copy)

    def line_finish(copies):
        for copy in copies[2:]:
            copy.wait_recv()

    def exchange_start(e, sums):
        place = lax.broadcasted_iota(jnp.int32, (8, 128), 0)
        tile = jnp.zeros((8, 128), f32)
        for i, x in enumerate(sums):
            tile = jnp.where(place == i, jnp.sum(x[:, :128] + x[:, 128:], axis=0, keepdims=True), tile)
        ex_src[e] = tile
        copies = [
            remote(ex_src.at[e], ex_dst.at[e, sector], e_send.at[e, d], e_recv.at[e, d], on_sector(d))
            for d in range(1, peers)
        ]
        ex_dst[e, sector] = tile
        pending.extend(copies)
        return copies

    def exchange_finish(e, copies, amount):
        for copy in copies:
            copy.wait_recv()
        total = ex_dst[e, 0]
        for d in range(1, peers):
            total = total + ex_dst[e, d]
        sums = jnp.sum(total, axis=1, keepdims=True)
        return [sums[i : i + 1] for i in range(amount)]

    mid = nstate - 2

    def mix(load, s):
        def step(i, _):
            span = pl.ds(pl.multiple_of(i * 16, 16), 16)
            block = load(s, slice(None), span).reshape(nstate * 16, n)
            out = mm(wk[...], block).astype(bf16).reshape(2, mid, 16, n)
            mixed[s, :, 1 : nstate - 1, span, :] = out
            return 0

        lax.fori_loop(0, n // 16, step, 0, unroll=True)
        for p in (0, nstate - 1):
            alone = load(s, p, slice(None)).astype(f32)
            for w in range(2):
                q = w * nstate + p
                mixed[s, w, p] = (alone * weights[q : q + 1, p : p + 1]).astype(bf16)

    def plain(ref):
        return lambda s, states, span: ref[s, states, span, :]

    def right_side(s, levels=range(5)):
        for level in levels:
            begin, finish = group_bounds[level]
            for w in range(2):
                def step(p, _):
                    half[s, p, w * n : (w + 1) * n, :] = mm_nt(mixed[s, w, p], rbuf[s + level, w]).astype(bf16)
                    return 0

                lax.fori_loop(begin, finish, step, 0, unroll=True)

    def left_of(finish, s, accs):
        def on_state(p, accs):
            values = finish(s, p, mm(env[s], half[s, p]))
            return tuple(a + fold(v) for a, v in zip(accs, values))

        return lax.fori_loop(0, nstate, on_state, accs, unroll=True)

    def zeros(sums):
        return tuple(jnp.zeros((8, n), f32) for _ in range(sums))

    def left_side(finish, sums):
        return lax.fori_loop(0, nsec, lambda s, accs: left_of(finish, s, accs), zeros(sums))

    ring_y = (g_send, g_recv, on_y(1), on_y(LINE - 1))
    ring_z = (t_send, t_recv, on_z(1), on_z(LINE - 1))
    copies = [line_send(gbuf, s, *ring_y) for s in range(nsec)]
    incoming[1].wait()
    for s in range(nsec):
        mask = mask_of(s)
        for w in range(2):
            rbuf[2 + s, w] = (rbuf[2 + s, w].astype(f32) * mask).astype(bf16)
    halo = (
        remote(rbuf.at[pl.ds(2, 2)], rbuf.at[pl.ds(0, 2)], r_send.at[0], r_recv.at[0], on_sector(1)),
        remote(rbuf.at[pl.ds(2, 2)], rbuf.at[pl.ds(4, 2)], r_send.at[1], r_recv.at[1], on_sector(peers - 1)),
    )

    def charge(p):
        return sum((p >= bound).astype(jnp.int32) for bound in (1, 5, 11, 15))

    shape = (2 * nstate, nstate)
    state_row = lax.broadcasted_iota(jnp.int32, shape, 0) % nstate
    state_col = lax.broadcasted_iota(jnp.int32, shape, 1)
    table = jnp.where(charge(state_row) == charge(state_col), weights[...], 0.0).astype(bf16)
    tall = (2 * mid * 16, 2 * nstate)
    which = lax.broadcasted_iota(jnp.int32, tall, 0) // 16
    which = which + jnp.where(which < mid, 1, 3)
    spread_rows = jnp.where(which == lax.broadcasted_iota(jnp.int32, tall, 1), 1.0, 0.0).astype(bf16)
    wide = (nstate, nstate * 16)
    spread_cols = jnp.where(
        lax.broadcasted_iota(jnp.int32, wide, 1) // 16 == lax.broadcasted_iota(jnp.int32, wide, 0), 1.0, 0.0
    ).astype(bf16)
    full = mm(mm(spread_rows, table).astype(bf16), spread_cols)
    big = full.shape
    same = lax.broadcasted_iota(jnp.int32, big, 0) % 16 == lax.broadcasted_iota(jnp.int32, big, 1) % 16
    wk[...] = jnp.where(same, full, 0.0).astype(bf16)

    incoming[2].wait()

    def masked(s, acc):
        mask = mask_of(s)

        def step(p, acc):
            value = u[s, p].astype(f32) * mask
            u[s, p] = value.astype(bf16)
            return acc + fold(value * value)

        return lax.fori_loop(0, nstate, step, acc, unroll=2)

    square = lax.fori_loop(0, nsec, masked, jnp.zeros((8, n), f32))
    started = exchange_start(0, [square])
    for s in range(nsec):
        line_forward(copies[s], gbuf, s, *ring_y)
        mix(plain(u), s)

    def slot(buf, at, j, s):
        return decode(buf.at[lax.rem(at - j + LINE, LINE), s])

    for s in range(nsec):
        line_finish(copies[s])
        factors = [split(slot(gbuf, y, j, s)) for j in range(LINE)]
        second = mm3(factors[0], factors[1])
        later = mm3(factors[2], factors[3])
        ypre[s] = second
        encode(mm3(split(second), split(later)), tbuf.at[0, s])
        copies[s] = line_send(tbuf, s, *ring_z)

    eye = jnp.where(rows == cols, 1.0, 0.0).astype(f32)

    def chosen(at, values):
        return jnp.where(
            at == 0, eye, jnp.where(at == 1, values[0], jnp.where(at == 2, values[1], values[2]))
        )

    for s in range(nsec):
        second = ypre[s]
        third = mm3(split(second), split(slot(gbuf, y, 2, s)))
        ypre[s] = chosen(y, (slot(gbuf, y, 0, s), second, third))
    for copy in halo:
        copy.wait_recv()
    pending.extend(halo)

    @pl.when(sector == 0)
    def _():
        rbuf[0:2] = jnp.zeros_like(rbuf[0:2])

    @pl.when(sector == peers - 1)
    def _():
        rbuf[4:6] = jnp.zeros_like(rbuf[4:6])

    incoming[3].wait()
    (uu,) = exchange_finish(0, started, 1)
    for s in range(nsec):
        right_side(s)
        line_forward(copies[s], tbuf, s, *ring_z)

    inv_count = 1.0 / count

    def row(x):
        return jnp.broadcast_to(x, (1, n))

    c0 = 1.0 / jnp.sqrt(uu * inv_count + eps)
    k_c0 = row(c0)

    def finish0(s, p, image):
        value = image * k_c0
        w0[s, p] = value.astype(bf16)
        return value * u[s, p].astype(f32), value * value

    sums = zeros(2)
    for s in range(nsec):
        line_finish(copies[s])
        near = [jnp.where(z > j, slot(tbuf, z, j, s), eye) for j in range(LINE - 1)]
        front = mm3(split(near[0]), split(near[1]))
        back = mm3(split(near[2]), split(ypre[s]))
        prefix = mm3(split(front), split(back))
        high, low = split(prefix)
        high_t, low_t = split(prefix.T)
        mask = mask_of(s)
        for w in range(2):
            base = (base_env[s, w].astype(f32) * mask).astype(bf16)
            inner = split(mm(base, high) + mm(base, low))
            left = mm3((high_t, low_t), inner).astype(bf16).astype(f32) * gates[s, w].astype(f32)
            env[s, :, w * n : (w + 1) * n] = left.astype(bf16)
        sums = left_of(finish0, s, sums)
    started = exchange_start(1, sums)
    mix(plain(w0), 0)
    right_side(0)
    mix(plain(w0), 1)
    right_side(1, range(3))
    s1, s2 = exchange_finish(1, started, 2)

    def inverse(x):
        return 1.0 / x

    def root(x):
        return jnp.sqrt(jnp.maximum(x, 0.0) * inv_count + eps)

    n00 = c0 * c0 * uu
    v0w0 = c0 * s1
    a0 = v0w0 * inv_count
    r0 = s2 - 2.0 * a0 * v0w0 + a0 * a0 * n00
    b0 = root(r0)
    i0 = inverse(b0)
    n11 = r0 * i0 * i0
    n01 = (v0w0 - a0 * n00) * i0

    shift = a0 * i0 * i0
    k_image, k_w0 = row(i0 * i0), row(shift)
    right_side(1, range(3, 5))

    def finish1(s, p, image):
        before = w0[s, p].astype(f32)
        value = image * k_image
        w1[s, p] = value.astype(bf16)
        return value * u[s, p].astype(f32), value * before, value * value

    started = exchange_start(2, left_side(finish1, 3))
    def shifted(s, states, span):
        value = w1[s, states, span, :].astype(f32) - w0[s, states, span, :].astype(f32) * k_w0
        return value.astype(bf16)

    for s in range(nsec):
        mix(shifted, s)
        right_side(s)

    def finish2(s, p, image):
        w2[s, p] = image.astype(bf16)
        older, before = w0[s, p].astype(f32), w1[s, p].astype(f32)
        return image * u[s, p].astype(f32), image * older, image * before, image * image

    last = exchange_start(3, left_side(finish2, 4))
    d0, e1, d2 = exchange_finish(2, started, 3)
    d0 = d0 - shift * s1
    d1 = e1 - shift * s2
    d2 = d2 - 2.0 * shift * e1 + shift * shift * s2
    v0w1 = c0 * d0 * b0
    v1w1 = d1 - a0 * c0 * d0
    w1w1 = d2 * b0 * b0
    a1 = v1w1 * inv_count
    r1 = w1w1 + a1 * a1 * n11 + b0 * b0 * n00 - 2.0 * a1 * v1w1 - 2.0 * b0 * v0w1 + 2.0 * a1 * b0 * n01
    b1 = root(r1)
    i1 = inverse(b1)
    n22 = r1 * i1 * i1
    n12 = (v1w1 - a1 * n11 - b0 * n01) * i1
    ratio = b0 * i1
    f0, f1, f2, f3 = exchange_finish(3, last, 4)
    f2 = f2 - shift * f1
    v0w2 = c0 * ratio * (f0 - a1 * d0 - s1)
    v1w2 = (ratio * (f1 - a1 * d1 - s2) - a0 * v0w2) * i0
    w1w2 = b0 * ratio * (f2 - a1 * d2 - d1)
    w2w2 = ratio * ratio * (f3 + a1 * a1 * d2 + s2 - 2.0 * a1 * f2 - 2.0 * f1 + 2.0 * a1 * d1)
    v2w2 = (w1w2 - a1 * v1w2 - b0 * v0w2) * i1
    a2 = v2w2 * inv_count
    r2 = w2w2 + a2 * a2 * n22 + b1 * b1 * n11 - 2.0 * a2 * v2w2 - 2.0 * b1 * v1w2 + 2.0 * a2 * b1 * n12
    b2 = root(r2)
    k3 = ritz[0, 3] / b2
    m2 = ritz[0, 2] - k3 * a2
    m1 = ritz[0, 1] - k3 * b1 - m2 * a1 * i1
    m0 = ritz[0, 0] - m2 * b0 * i1 - m1 * a0 * i0
    k_last = k3 * ratio
    k_next = m2 * ratio - k_last * a1
    lane = lax.broadcasted_iota(jnp.int32, (1, 128), 1)
    for i, (x, y0, y1) in enumerate(((a0, a1, a2), (b0, b1, b2))):
        tri_out[i : i + 1, :] = jnp.where(lane == 0, x, jnp.where(lane == 1, y0, y1))
    for i, x in enumerate((m0 * c0, m1 * i0 - k_last - k_next * shift, k_next, k_last)):
        coef_out[i : i + 1, :] = row(x)
    for copy in pending:
        copy.wait_send()


def combine(coef, tri, u, w0, w1, w2, psi, tri_out, block, sems):
    tri_out[0] = tri[0:2, 0:3]
    parts = sems.shape[0]
    span = u.shape[0] // parts
    weights = [coef[i : i + 1, :] for i in range(4)]
    copies = []
    for part in range(parts):
        rows = pl.ds(part * span, span)

        def step(i, _):
            some = pl.ds(pl.multiple_of(part * span + i * 64, 64), 64)
            total = u[some, :].astype(f32) * weights[0]
            total = total + w0[some, :].astype(f32) * weights[1]
            total = total + w1[some, :].astype(f32) * weights[2]
            block[some, :] = total + w2[some, :].astype(f32) * weights[3]
            return 0

        lax.fori_loop(0, span // 64, step, 0, unroll=4)
        copy = pltpu.make_async_copy(block.at[rows], psi.at[rows], sems.at[part])
        copy.start()
        copies.append(copy)
    for copy in copies:
        copy.wait()


def on_device(peers, theta, env_left0, transfer, env_right, mpo_weights, term_mask, block_sizes, ritz):
    _, nsec, nstate, n, _ = theta.shape
    field = pltpu.VMEM((nsec, nstate, n, n), bf16)
    smem = pl.BlockSpec(memory_space=pltpu.SMEM)
    vmem = pl.BlockSpec(memory_space=pltpu.VMEM)
    hbm = pl.BlockSpec(memory_space=pl.ANY)
    dma = pltpu.SemaphoreType.DMA
    code = pltpu.VMEM((4, nsec, n + 16, n), jnp.int16)
    u, w0, w1, w2, tri, coef = pl.pallas_call(
        kernel,
        out_shape=(field, field, field, field, pltpu.VMEM((8, 128), f32), pltpu.VMEM((8, n), f32)),
        in_specs=[smem, smem, smem, hbm, hbm, hbm, hbm, vmem],
        out_specs=(vmem,) * 6,
        scratch_shapes=[
            code, code,
            pltpu.VMEM((nsec + 4, 2, n, n), bf16),
            pltpu.VMEM((2 * (nstate - 2) * 16, nstate * 16), bf16),
            pltpu.VMEM((nsec, n, 2 * n), bf16),
            pltpu.VMEM((nsec, n, n), f32),
            pltpu.VMEM((nsec, 2, nstate, n, n), bf16),
            pltpu.VMEM((nsec, nstate, 2 * n, n), bf16),
            pltpu.VMEM((4, 8, 128), f32),
            pltpu.VMEM((4, peers, 8, 128), f32),
            pltpu.VMEM((nsec, n, n), f32),
            pltpu.VMEM((nsec, 2, n, n), bf16),
            dma((4,)), dma((nsec, 6)), dma((nsec, 6)), dma((nsec, 6)), dma((nsec, 6)),
            dma((2,)), dma((2,)), dma((4, peers)), dma((4, peers)),
        ],
        compiler_params=pltpu.CompilerParams(
            collective_id=0, has_side_effects=True, vmem_limit_bytes=40 * 2**20
        ),
    )(
        block_sizes, term_mask, ritz, theta, env_left0, transfer, env_right,
        mpo_weights.reshape(2 * nstate, nstate),
    )
    total = nsec * nstate * n
    flat = [x.reshape(total, n) for x in (u, w0, w1, w2)]
    parts = 16
    psi, tridiag = pl.pallas_call(
        combine,
        out_shape=(jax.ShapeDtypeStruct((total, n), f32), jax.ShapeDtypeStruct((1, 2, 3), f32)),
        in_specs=[vmem] * 6,
        out_specs=(hbm, vmem),
        scratch_shapes=[pltpu.VMEM((total, n), f32), dma((parts,))],
        compiler_params=pltpu.CompilerParams(vmem_limit_bytes=24 * 2**20),
    )(coef, tri, *flat)
    return psi.reshape(theta.shape), tridiag


def solution(mesh):
    in_specs = (
        P("chain", "sector", None, None, None),
        P("sector", None, None, None),
        P("chain", "sector", None, None),
        P("chain", "sector", None, None, None),
        P(),
        P("sector", None),
        P("sector"),
        P("chain", None),
    )
    out_specs = (P("chain", "sector", None, None, None), P("chain", None, None))
    return jax.shard_map(
        functools.partial(on_device, mesh.shape["sector"]),
        mesh=mesh, in_specs=in_specs, out_specs=out_specs, check_vma=False,
    )
```

```python
import functools

import jax
import jax.numpy as jnp
from jax import lax
from jax.experimental import pallas as pl
from jax.experimental.pallas import tpu as pltpu
from jax.sharding import PartitionSpec as P

f32, bf16 = jnp.float32, jnp.bfloat16
MESH = pl.DeviceIdType.MESH
group_bounds = [(0, 1), (1, 5), (5, 11), (11, 15), (15, 16)]
eps = 1e-6
LINE = 4
TOP = 32767.0


def split(x):
    high = x.astype(bf16)
    return high, (x - high.astype(f32)).astype(bf16)


def mm(a, b):
    return jnp.dot(a, b, preferred_element_type=f32)


def mm_nt(a, b):
    return lax.dot_general(a, b, (((1,), (1,)), ((), ())), preferred_element_type=f32)


def mm3(a, b):
    return mm(a[0], b[0]) + mm(a[0], b[1]) + mm(a[1], b[0])


def encode(x, ref):
    n = x.shape[0]
    top = jnp.max(jnp.abs(x), axis=0, keepdims=True)
    power = jnp.ceil(jnp.log2(jnp.maximum(top, 1e-35)) + 0.01)
    code = jnp.round(x * (jnp.exp2(-power) * TOP))
    ref[0:n] = code.astype(jnp.int32).astype(jnp.int16)
    ref[n : n + 16] = jnp.broadcast_to(power, (16, x.shape[1])).astype(jnp.int32).astype(jnp.int16)


def decode(ref):
    n = ref.shape[0] - 16
    power = ref[n : n + 16].astype(jnp.int32).astype(f32)[0:1]
    return ref[0:n].astype(jnp.int32).astype(f32) * (jnp.exp2(power) * (1.0 / TOP))


def fold(x):
    return jnp.sum(x.reshape(-1, 8, x.shape[-1]), axis=0)


def kernel(
    sizes, gates, ritz, theta, env_left, transfer, env_right, weights,
    u, w0, w1, w2, tri_out, coef_out,
    gbuf, tbuf, rbuf, wk, env, ypre, mixed, half, ex_src, ex_dst, factor, base_env,
    in_sem, g_send, g_recv, t_send, t_recv, r_send, r_recv, e_send, e_recv,
):
    nsec, nstate, n = u.shape[0], u.shape[1], u.shape[-1]
    chain, sector = lax.axis_index("chain"), lax.axis_index("sector")
    peers = ex_dst.shape[1]
    count = float(peers * nsec * nstate * n * n)
    z, y = chain // LINE, lax.rem(chain, LINE)

    def on_y(d):
        return (z * LINE + lax.rem(y + d, LINE), sector)

    def on_z(d):
        return (lax.rem(z + d, LINE) * LINE + y, sector)

    def on_sector(d):
        return (chain, lax.rem(sector + d, peers))

    barrier = pltpu.get_barrier_semaphore()
    others = [on_y(1), on_y(LINE - 1), on_z(1), on_z(LINE - 1)] + [on_sector(d) for d in range(1, peers)]
    for other in others:
        pl.semaphore_signal(barrier, inc=1, device_id=other, device_id_type=MESH)

    incoming = [
        pltpu.make_async_copy(src, dst, in_sem.at[i])
        for i, (src, dst) in enumerate((
            (transfer.at[0], factor), (env_right.at[0], rbuf.at[pl.ds(2, 2)]), (theta.at[0], u), (env_left, base_env),
        ))
    ]
    for copy in incoming:
        copy.start()
    rows = lax.broadcasted_iota(jnp.int32, (n, n), 0)
    cols = lax.broadcasted_iota(jnp.int32, (n, n), 1)

    def mask_of(s):
        return jnp.where((rows < sizes[s]) & (cols < sizes[s]), 1.0, 0.0).astype(f32)

    incoming[0].wait()
    for s in range(nsec):
        encode(factor[s] * mask_of(s), gbuf.at[0, s])
    pl.semaphore_wait(barrier, len(others))

    def remote(src, dst, send, recv, device):
        copy = pltpu.make_async_remote_copy(
            src_ref=src, dst_ref=dst, send_sem=send, recv_sem=recv,
            device_id=device, device_id_type=MESH,
        )
        copy.start()
        return copy

    pending = []
    upper, lower = pl.ds(0, n // 2), pl.ds(n // 2, n // 2 + 16)

    def line_send(buf, s, send, recv, onward, back):
        plan = ((1, upper, onward), (3, lower, back), (1, lower, onward), (3, upper, back))
        copies = [
            remote(buf.at[0, s, part], buf.at[place, s, part], send.at[s, i], recv.at[s, i], device)
            for i, (place, part, device) in enumerate(plan)
        ]
        pending.extend(copies)
        return copies

    def line_forward(copies, buf, s, send, recv, onward, back):
        for i, (place, part, device) in enumerate(((1, upper, onward), (3, lower, back))):
            copies[i].wait_recv()
            copy = remote(buf.at[place, s, part], buf.at[2, s, part], send.at[s, 4 + i], recv.at[s, 4 + i], device)
            copies.append(copy)
            pending.append(copy)

    def line_finish(copies):
        for copy in copies[2:]:
            copy.wait_recv()

    def exchange_start(e, sums):
        place = lax.broadcasted_iota(jnp.int32, (8, 128), 0)
        tile = jnp.zeros((8, 128), f32)
        for i, x in enumerate(sums):
            tile = jnp.where(place == i, jnp.sum(x[:, :128] + x[:, 128:], axis=0, keepdims=True), tile)
        ex_src[e] = tile
        copies = [
            remote(ex_src.at[e], ex_dst.at[e, sector], e_send.at[e, d], e_recv.at[e, d], on_sector(d))
            for d in sorted(range(1, peers), key=lambda d: -min(d, peers - d))
        ]
        ex_dst[e, sector] = tile
        pending.extend(copies)
        return copies

    def exchange_finish(e, copies, amount):
        for copy in copies:
            copy.wait_recv()
        total = ex_dst[e, 0]
        for d in range(1, peers):
            total = total + ex_dst[e, d]
        sums = jnp.sum(total, axis=1, keepdims=True)
        return [sums[i : i + 1] for i in range(amount)]

    mid = nstate - 2

    def mix(load, s):
        def step(i, _):
            span = pl.ds(pl.multiple_of(i * 16, 16), 16)
            block = load(s, slice(None), span).reshape(nstate * 16, n)
            out = mm(wk[...], block).astype(bf16).reshape(2, mid, 16, n)
            mixed[s, :, 1 : nstate - 1, span, :] = out
            return 0

        lax.fori_loop(0, n // 16, step, 0, unroll=True)
        for p in (0, nstate - 1):
            alone = load(s, p, slice(None)).astype(f32)
            for w in range(2):
                q = w * nstate + p
                mixed[s, w, p] = (alone * weights[q : q + 1, p : p + 1]).astype(bf16)

    def plain(ref):
        return lambda s, states, span: ref[s, states, span, :]

    def right_side(s, levels=range(5)):
        for level in levels:
            begin, finish = group_bounds[level]
            for w in range(2):
                def step(p, _):
                    half[s, p, w * n : (w + 1) * n, :] = mm_nt(mixed[s, w, p], rbuf[s + level, w]).astype(bf16)
                    return 0

                lax.fori_loop(begin, finish, step, 0, unroll=True)

    def left_of(finish, s, accs):
        def on_state(p, accs):
            values = finish(s, p, mm(env[s], half[s, p]))
            return tuple(a + fold(v) for a, v in zip(accs, values))

        return lax.fori_loop(0, nstate, on_state, accs, unroll=True)

    def zeros(sums):
        return tuple(jnp.zeros((8, n), f32) for _ in range(sums))

    def left_side(finish, sums):
        return lax.fori_loop(0, nsec, lambda s, accs: left_of(finish, s, accs), zeros(sums))

    ring_y = (g_send, g_recv, on_y(1), on_y(LINE - 1))
    ring_z = (t_send, t_recv, on_z(1), on_z(LINE - 1))
    copies = [line_send(gbuf, s, *ring_y) for s in range(nsec)]
    incoming[1].wait()
    for s in range(nsec):
        mask = mask_of(s)
        for w in range(2):
            rbuf[2 + s, w] = (rbuf[2 + s, w].astype(f32) * mask).astype(bf16)
    halo = (
        remote(rbuf.at[pl.ds(2, 2)], rbuf.at[pl.ds(0, 2)], r_send.at[0], r_recv.at[0], on_sector(1)),
        remote(rbuf.at[pl.ds(2, 2)], rbuf.at[pl.ds(4, 2)], r_send.at[1], r_recv.at[1], on_sector(peers - 1)),
    )

    def charge(p):
        return sum((p >= bound).astype(jnp.int32) for bound in (1, 5, 11, 15))

    shape = (2 * nstate, nstate)
    state_row = lax.broadcasted_iota(jnp.int32, shape, 0) % nstate
    state_col = lax.broadcasted_iota(jnp.int32, shape, 1)
    table = jnp.where(charge(state_row) == charge(state_col), weights[...], 0.0).astype(bf16)
    tall = (2 * mid * 16, 2 * nstate)
    which = lax.broadcasted_iota(jnp.int32, tall, 0) // 16
    which = which + jnp.where(which < mid, 1, 3)
    spread_rows = jnp.where(which == lax.broadcasted_iota(jnp.int32, tall, 1), 1.0, 0.0).astype(bf16)
    wide = (nstate, nstate * 16)
    spread_cols = jnp.where(
        lax.broadcasted_iota(jnp.int32, wide, 1) // 16 == lax.broadcasted_iota(jnp.int32, wide, 0), 1.0, 0.0
    ).astype(bf16)
    full = mm(mm(spread_rows, table).astype(bf16), spread_cols)
    big = full.shape
    same = lax.broadcasted_iota(jnp.int32, big, 0) % 16 == lax.broadcasted_iota(jnp.int32, big, 1) % 16
    wk[...] = jnp.where(same, full, 0.0).astype(bf16)

    incoming[2].wait()

    def masked(s, acc):
        mask = mask_of(s)

        def step(p, acc):
            value = u[s, p].astype(f32) * mask
            u[s, p] = value.astype(bf16)
            return acc + fold(value * value)

        return lax.fori_loop(0, nstate, step, acc, unroll=2)

    square = lax.fori_loop(0, nsec, masked, jnp.zeros((8, n), f32))
    started = exchange_start(0, [square])
    for s in range(nsec):
        line_forward(copies[s], gbuf, s, *ring_y)
        mix(plain(u), s)

    def slot(buf, at, j, s):
        return decode(buf.at[lax.rem(at - j + LINE, LINE), s])

    for s in range(nsec):
        line_finish(copies[s])
        factors = [split(slot(gbuf, y, j, s)) for j in range(LINE)]
        second = mm3(factors[0], factors[1])
        later = mm3(factors[2], factors[3])
        ypre[s] = second
        encode(mm3(split(second), split(later)), tbuf.at[0, s])
        copies[s] = line_send(tbuf, s, *ring_z)

    eye = jnp.where(rows == cols, 1.0, 0.0).astype(f32)

    def chosen(at, values):
        return jnp.where(
            at == 0, eye, jnp.where(at == 1, values[0], jnp.where(at == 2, values[1], values[2]))
        )

    for s in range(nsec):
        second = ypre[s]
        third = mm3(split(second), split(slot(gbuf, y, 2, s)))
        ypre[s] = chosen(y, (slot(gbuf, y, 0, s), second, third))
    for copy in halo:
        copy.wait_recv()
    pending.extend(halo)

    @pl.when(sector == 0)
    def _():
        rbuf[0:2] = jnp.zeros_like(rbuf[0:2])

    @pl.when(sector == peers - 1)
    def _():
        rbuf[4:6] = jnp.zeros_like(rbuf[4:6])

    incoming[3].wait()
    (uu,) = exchange_finish(0, started, 1)
    for s in range(nsec):
        right_side(s)
        line_forward(copies[s], tbuf, s, *ring_z)

    inv_count = 1.0 / count

    def row(x):
        return jnp.broadcast_to(x, (1, n))

    c0 = 1.0 / jnp.sqrt(uu * inv_count + eps)
    k_c0 = row(c0)

    def finish0(s, p, image):
        value = image * k_c0
        w0[s, p] = value.astype(bf16)
        return value * u[s, p].astype(f32), value * value

    sums = zeros(2)
    for s in range(nsec):
        line_finish(copies[s])
        near = [jnp.where(z > j, slot(tbuf, z, j, s), eye) for j in range(LINE - 1)]
        front = mm3(split(near[0]), split(near[1]))
        back = mm3(split(near[2]), split(ypre[s]))
        prefix = mm3(split(front), split(back))
        high, low = split(prefix)
        high_t, low_t = split(prefix.T)
        mask = mask_of(s)
        for w in range(2):
            base = (base_env[s, w].astype(f32) * mask).astype(bf16)
            inner = split(mm(base, high) + mm(base, low))
            left = mm3((high_t, low_t), inner).astype(bf16).astype(f32) * gates[s, w].astype(f32)
            env[s, :, w * n : (w + 1) * n] = left.astype(bf16)
        sums = left_of(finish0, s, sums)
    started = exchange_start(1, sums)
    mix(plain(w0), 0)
    right_side(0)
    mix(plain(w0), 1)
    right_side(1, range(3))
    s1, s2 = exchange_finish(1, started, 2)

    def inverse(x):
        return 1.0 / x

    def root(x):
        return jnp.sqrt(jnp.maximum(x, 0.0) * inv_count + eps)

    n00 = c0 * c0 * uu
    v0w0 = c0 * s1
    a0 = v0w0 * inv_count
    r0 = s2 - 2.0 * a0 * v0w0 + a0 * a0 * n00
    b0 = root(r0)
    i0 = inverse(b0)
    n11 = r0 * i0 * i0
    n01 = (v0w0 - a0 * n00) * i0

    shift = a0 * i0 * i0
    k_image, k_w0 = row(i0 * i0), row(shift)
    right_side(1, range(3, 5))

    def finish1(s, p, image):
        before = w0[s, p].astype(f32)
        value = image * k_image
        w1[s, p] = value.astype(bf16)
        return value * u[s, p].astype(f32), value * before, value * value

    started = exchange_start(2, left_side(finish1, 3))
    def shifted(s, states, span):
        value = w1[s, states, span, :].astype(f32) - w0[s, states, span, :].astype(f32) * k_w0
        return value.astype(bf16)

    for s in range(nsec):
        mix(shifted, s)
        right_side(s)

    def finish2(s, p, image):
        w2[s, p] = image.astype(bf16)
        older, before = w0[s, p].astype(f32), w1[s, p].astype(f32)
        return image * u[s, p].astype(f32), image * older, image * before, image * image

    last = exchange_start(3, left_side(finish2, 4))
    for copy in pending[: -len(last)]:
        copy.wait_send()
    d0, e1, d2 = exchange_finish(2, started, 3)
    d0 = d0 - shift * s1
    d1 = e1 - shift * s2
    d2 = d2 - 2.0 * shift * e1 + shift * shift * s2
    v0w1 = c0 * d0 * b0
    v1w1 = d1 - a0 * c0 * d0
    w1w1 = d2 * b0 * b0
    a1 = v1w1 * inv_count
    r1 = w1w1 + a1 * a1 * n11 + b0 * b0 * n00 - 2.0 * a1 * v1w1 - 2.0 * b0 * v0w1 + 2.0 * a1 * b0 * n01
    b1 = root(r1)
    i1 = inverse(b1)
    n22 = r1 * i1 * i1
    n12 = (v1w1 - a1 * n11 - b0 * n01) * i1
    ratio = b0 * i1
    f0, f1, f2, f3 = exchange_finish(3, last, 4)
    f2 = f2 - shift * f1
    v0w2 = c0 * ratio * (f0 - a1 * d0 - s1)
    v1w2 = (ratio * (f1 - a1 * d1 - s2) - a0 * v0w2) * i0
    w1w2 = b0 * ratio * (f2 - a1 * d2 - d1)
    w2w2 = ratio * ratio * (f3 + a1 * a1 * d2 + s2 - 2.0 * a1 * f2 - 2.0 * f1 + 2.0 * a1 * d1)
    v2w2 = (w1w2 - a1 * v1w2 - b0 * v0w2) * i1
    a2 = v2w2 * inv_count
    r2 = w2w2 + a2 * a2 * n22 + b1 * b1 * n11 - 2.0 * a2 * v2w2 - 2.0 * b1 * v1w2 + 2.0 * a2 * b1 * n12
    b2 = root(r2)
    k3 = ritz[0, 3] / b2
    m2 = ritz[0, 2] - k3 * a2
    m1 = ritz[0, 1] - k3 * b1 - m2 * a1 * i1
    m0 = ritz[0, 0] - m2 * b0 * i1 - m1 * a0 * i0
    k_last = k3 * ratio
    k_next = m2 * ratio - k_last * a1
    lane = lax.broadcasted_iota(jnp.int32, (1, 128), 1)
    for i, (x, y0, y1) in enumerate(((a0, a1, a2), (b0, b1, b2))):
        tri_out[i : i + 1, :] = jnp.where(lane == 0, x, jnp.where(lane == 1, y0, y1))
    for i, x in enumerate((m0 * c0, m1 * i0 - k_last - k_next * shift, k_next, k_last)):
        coef_out[i : i + 1, :] = row(x)
    for copy in last:
        copy.wait_send()


def combine(coef, tri, u, w0, w1, w2, psi, tri_out, block, sems):
    tri_out[0] = tri[0:2, 0:3]
    parts = sems.shape[0]
    span = u.shape[0] // parts
    weights = [coef[i : i + 1, :] for i in range(4)]
    copies = []
    for part in range(parts):
        rows = pl.ds(part * span, span)

        def step(i, _):
            some = pl.ds(pl.multiple_of(part * span + i * 64, 64), 64)
            total = u[some, :].astype(f32) * weights[0]
            total = total + w0[some, :].astype(f32) * weights[1]
            total = total + w1[some, :].astype(f32) * weights[2]
            block[some, :] = total + w2[some, :].astype(f32) * weights[3]
            return 0

        lax.fori_loop(0, span // 64, step, 0, unroll=4)
        copy = pltpu.make_async_copy(block.at[rows], psi.at[rows], sems.at[part])
        copy.start()
        copies.append(copy)
    for copy in copies:
        copy.wait()


def on_device(peers, theta, env_left0, transfer, env_right, mpo_weights, term_mask, block_sizes, ritz):
    _, nsec, nstate, n, _ = theta.shape
    field = pltpu.VMEM((nsec, nstate, n, n), bf16)
    smem = pl.BlockSpec(memory_space=pltpu.SMEM)
    vmem = pl.BlockSpec(memory_space=pltpu.VMEM)
    hbm = pl.BlockSpec(memory_space=pl.ANY)
    dma = pltpu.SemaphoreType.DMA
    code = pltpu.VMEM((4, nsec, n + 16, n), jnp.int16)
    u, w0, w1, w2, tri, coef = pl.pallas_call(
        kernel,
        out_shape=(field, field, field, field, pltpu.VMEM((8, 128), f32), pltpu.VMEM((8, n), f32)),
        in_specs=[smem, smem, smem, hbm, hbm, hbm, hbm, vmem],
        out_specs=(vmem,) * 6,
        scratch_shapes=[
            code, code,
            pltpu.VMEM((nsec + 4, 2, n, n), bf16),
            pltpu.VMEM((2 * (nstate - 2) * 16, nstate * 16), bf16),
            pltpu.VMEM((nsec, n, 2 * n), bf16),
            pltpu.VMEM((nsec, n, n), f32),
            pltpu.VMEM((nsec, 2, nstate, n, n), bf16),
            pltpu.VMEM((nsec, nstate, 2 * n, n), bf16),
            pltpu.VMEM((4, 8, 128), f32),
            pltpu.VMEM((4, peers, 8, 128), f32),
            pltpu.VMEM((nsec, n, n), f32),
            pltpu.VMEM((nsec, 2, n, n), bf16),
            dma((4,)), dma((nsec, 6)), dma((nsec, 6)), dma((nsec, 6)), dma((nsec, 6)),
            dma((2,)), dma((2,)), dma((4, peers)), dma((4, peers)),
        ],
        compiler_params=pltpu.CompilerParams(
            collective_id=0, has_side_effects=True, vmem_limit_bytes=40 * 2**20
        ),
    )(
        block_sizes, term_mask, ritz, theta, env_left0, transfer, env_right,
        mpo_weights.reshape(2 * nstate, nstate),
    )
    total = nsec * nstate * n
    flat = [x.reshape(total, n) for x in (u, w0, w1, w2)]
    parts = 32
    psi, tridiag = pl.pallas_call(
        combine,
        out_shape=(jax.ShapeDtypeStruct((total, n), f32), jax.ShapeDtypeStruct((1, 2, 3), f32)),
        in_specs=[vmem] * 6,
        out_specs=(hbm, vmem),
        scratch_shapes=[pltpu.VMEM((total, n), f32), dma((parts,))],
        compiler_params=pltpu.CompilerParams(vmem_limit_bytes=24 * 2**20),
    )(coef, tri, *flat)
    return psi.reshape(theta.shape), tridiag


def solution(mesh):
    in_specs = (
        P("chain", "sector", None, None, None),
        P("sector", None, None, None),
        P("chain", "sector", None, None),
        P("chain", "sector", None, None, None),
        P(),
        P("sector", None),
        P("sector"),
        P("chain", None),
    )
    out_specs = (P("chain", "sector", None, None, None), P("chain", None, None))
    return jax.shard_map(
        functools.partial(on_device, mesh.shape["sector"]),
        mesh=mesh, in_specs=in_specs, out_specs=out_specs, check_vma=False,
    )
```
